256 devices in a mesh: row: 32 (over x_hi, z, core), col: 8 (over y, x_lo).
Axes of the slice: x: 4 (x_hi: 2, x_lo: 2; x = x_hi * 2 + x_lo), y: 4, z: 8, core: 2. Of those that a mesh axis runs over, the one named last changes fastest.
Arguments:
- pair: bfloat16 [1024, 1024, 128], P('row', 'col'), may hold values from -6 to 6
- ln_in_gain: float32 [128], replicated, may hold values from 0.1 to 1.9
- proj_left: bfloat16 [128, 256], replicated, may hold values from -0.5 to 0.5
- proj_right: bfloat16 [128, 256], replicated, may hold values from -0.5 to 0.5
- gate_weight: bfloat16 [128, 128], replicated, may hold values from -0.5 to 0.5
- ln_out_gain: float32 [128], replicated, may hold values from 0.1 to 1.9
- out_weight: bfloat16 [128, 128], replicated, may hold values from -0.5 to 0.5
Outputs:
- update: bfloat16 [1024, 1024, 128], P('row', 'col')
The draws below stay inside these ranges and needn't reach their ends.
All inputs are finite; a program needn't handle non-finite values.
Results may differ from the reference program's by a relative error of at most 0.0083.
Values may be sent and summed in bfloat16 or wider, within the bound.
No kernel may reach another device: no remote copies, remote signals or barrier semaphores. Data moves between devices by JAX's collectives and lax.ppermute only.
A program may use at most 64 MiB of HBM per device.

```python
import math
import jax
import jax.numpy as jnp
from jax import lax

CHANNELS = 128
HIDDEN_SIZE = 128
NTOK = 1024


def steps_of(key, extent, split, smallest, top_value):
    level, own = 1.0, jax.random.fold_in(key, 6)
    for dim, blocks in split:
        steps = jnp.exp(jax.random.uniform(jax.random.fold_in(own, dim), (blocks,), jnp.float32, smallest / len(split), top_value / len(split)))
        level = level * jnp.repeat(steps, extent[dim] // blocks).reshape([-1 if axis == dim else 1 for axis in range(len(extent))])
    return level


def normal_values(own_key, shape, width, most, split=(), held_as=jnp.bfloat16):
    result = jax.random.normal(own_key, shape, jnp.float32) * width
    if len(split) > 0:
        result = steps_of(own_key, shape, split, -0.22, 0.18) * result
    return jnp.clip(result, min=-most, max=most).astype(held_as)


def setup_inputs(seed: int = 0) -> dict:
    arg_keys = jax.random.split(jax.random.key(seed), 8)
    pair = normal_values(arg_keys[0], (NTOK, NTOK, CHANNELS), 1.0, 6.0, ((0, 32), (1, 8)))
    ln_in_gain = jnp.clip(1.0 + 0.18 * jax.random.normal(arg_keys[1], (CHANNELS,), jnp.float32), 0.1, 1.9)
    proj_left = normal_values(arg_keys[2], (CHANNELS, 2 * HIDDEN_SIZE), CHANNELS ** -0.5, 0.5)
    proj_right = normal_values(arg_keys[3], (CHANNELS, 2 * HIDDEN_SIZE), CHANNELS ** -0.5, 0.5)
    gate_weight = normal_values(arg_keys[4], (CHANNELS, CHANNELS), CHANNELS ** -0.5, 0.5)
    ln_out_gain = jnp.clip(1.0 + 0.18 * jax.random.normal(arg_keys[5], (HIDDEN_SIZE,), jnp.float32), 0.1, 1.9)
    out_weight = normal_values(arg_keys[6], (HIDDEN_SIZE, CHANNELS), HIDDEN_SIZE ** -0.5, 0.5)
    return {"pair": pair, "ln_in_gain": ln_in_gain, "proj_left": proj_left, "proj_right": proj_right, "gate_weight": gate_weight, "ln_out_gain": ln_out_gain, "out_weight": out_weight}


def layer_norm(values, scale_gain, dimension):
    average = lax.optimization_barrier(jnp.mean(values, axis=dimension, keepdims=True))
    centered = values - average
    spread = lax.optimization_barrier(jnp.mean(centered * centered, axis=dimension, keepdims=True))
    return centered * lax.rsqrt(spread + 1e-05) * scale_gain

def reference(pair, ln_in_gain, proj_left, proj_right, gate_weight, ln_out_gain, out_weight):
    block_rows = math.gcd(NTOK, 64)
    block_count = NTOK // block_rows
    left_wide = proj_left.astype(jnp.float32)
    right_wide = proj_right.astype(jnp.float32)
    gate_wide = gate_weight.astype(jnp.float32)
    out_wide = out_weight.astype(jnp.float32)

    def normalize(stripe):
        return layer_norm(stripe.astype(jnp.float32), ln_in_gain, -1).astype(jnp.bfloat16).astype(jnp.float32)

    def project_rows(stripe):
        normed = normalize(stripe)
        left_both = jnp.einsum('rcd,de->rce', normed, left_wide)
        right_both = jnp.einsum('rcd,de->rce', normed, right_wide)
        left_side = (jax.nn.sigmoid(left_both[..., :HIDDEN_SIZE]) * left_both[..., HIDDEN_SIZE:]).astype(jnp.bfloat16)
        right_side = (jax.nn.sigmoid(right_both[..., :HIDDEN_SIZE]) * right_both[..., HIDDEN_SIZE:]).astype(jnp.bfloat16)
        return (left_side, right_side)
    stripes = pair.reshape(block_count, block_rows, NTOK, CHANNELS)
    left_side, right_side = lax.map(project_rows, stripes)
    left_side = jnp.transpose(left_side.reshape(NTOK, NTOK, HIDDEN_SIZE), (2, 0, 1))
    right_side = jnp.transpose(right_side.reshape(NTOK, NTOK, HIDDEN_SIZE), (2, 0, 1))
    group_count = HIDDEN_SIZE // 8

    def triangle(operands):
        first, second = operands
        return jnp.einsum('hik,hjk->hij', first.astype(jnp.float32), second.astype(jnp.float32)).astype(jnp.bfloat16)
    product = lax.map(triangle, (left_side.reshape(group_count, 8, NTOK, NTOK), right_side.reshape(group_count, 8, NTOK, NTOK)))
    product = product.reshape(HIDDEN_SIZE, block_count, block_rows, NTOK)
    product = jnp.transpose(product, (1, 0, 2, 3))

    def finish(operands):
        piece_product, stripe = operands
        normed = normalize(stripe)
        gating = jax.nn.sigmoid(jnp.einsum('rcd,de->rce', normed, gate_wide))
        product_norm = layer_norm(piece_product.astype(jnp.float32), ln_out_gain.reshape(-1, 1, 1), 0)
        product_norm = product_norm.astype(jnp.bfloat16).astype(jnp.float32)
        projected = jnp.einsum('hrc,hd->rcd', product_norm, out_wide)
        return (gating * projected).astype(jnp.bfloat16)
    update = lax.map(finish, (product, stripes))
    return update.reshape(NTOK, NTOK, CHANNELS)
```

```python
import jax
import jax.numpy as jnp
from jax import lax
from jax.sharding import PartitionSpec as P


def layer_norm(values, scale_gain, dimension):
    average = jnp.mean(values, axis=dimension, keepdims=True)
    centered = values - average
    spread = jnp.mean(centered * centered, axis=dimension, keepdims=True)
    return centered * lax.rsqrt(spread + 1e-05) * scale_gain


def gated_pair(normed, weights, width):
    both = jnp.einsum("rcd,de->erc", normed, weights, preferred_element_type=jnp.float32)
    return (jax.nn.sigmoid(both[:width]) * both[width:]).astype(jnp.bfloat16)


def shards(rows, cols, pair, ln_in_gain, proj_left, proj_right, gate_weight, ln_out_gain, out_weight):
    width = out_weight.shape[0]
    here_i, here_k = pair.shape[0], pair.shape[1]
    half = here_i // 2
    chips = rows // 2
    normed = layer_norm(pair.astype(jnp.float32), ln_in_gain, -1).astype(jnp.bfloat16)
    left_side = gated_pair(normed, proj_left, width)
    right_side = gated_pair(normed, proj_right, width)
    gating = jax.nn.sigmoid(
        jnp.einsum("rcd,de->rce", normed, gate_weight, preferred_element_type=jnp.float32)
    )

    def by_device(side):
        side = side.reshape(chips, cols, 2, half, here_k)
        return jnp.swapaxes(side, 1, 2).reshape(rows * cols, half, here_k)

    sent = jnp.stack([by_device(left_side), by_device(right_side)], axis=1)
    got = lax.all_to_all(sent, ("row", "col"), split_axis=0, concat_axis=0, tiled=True)

    def panel(one):
        one = one.reshape(rows, cols, half, here_k)
        return jnp.swapaxes(one, 1, 2).reshape(rows, half, cols * here_k)

    left_panel, right_own = panel(got[:, 0]), panel(got[:, 1])
    right_other = lax.ppermute(right_own, "row", [(r, r ^ 1) for r in range(rows)])
    first_core = lax.axis_index("row") % 2 == 0
    right_panel = jnp.stack(
        [
            jnp.where(first_core, right_own, right_other),
            jnp.where(first_core, right_other, right_own),
        ],
        axis=1,
    ).reshape(rows * here_i, cols * here_k)
    product = jnp.einsum(
        "rik,jk->rij", left_panel, right_panel, preferred_element_type=jnp.float32
    ).astype(jnp.bfloat16)
    product = product.reshape(rows, half, cols, here_k)
    product = jnp.swapaxes(product, 1, 2).reshape(rows * cols, half, here_k)
    back = lax.all_to_all(product, ("row", "col"), split_axis=0, concat_axis=0, tiled=True)
    by_owner = jnp.swapaxes(back.reshape(chips, 2, cols, half, here_k), 1, 2)
    by_owner = by_owner.reshape(width, here_i, here_k)
    product_norm = layer_norm(
        by_owner.astype(jnp.float32), ln_out_gain.reshape(-1, 1, 1), 0
    ).astype(jnp.bfloat16)
    projected = jnp.einsum(
        "hrc,hd->rcd", product_norm, out_weight, preferred_element_type=jnp.float32
    )
    return (gating * projected).astype(jnp.bfloat16)


def solution(mesh):
    rows, cols = mesh.shape["row"], mesh.shape["col"]
    in_specs = (P("row", "col", None), P(), P(), P(), P(), P(), P())
    out_specs = P("row", "col", None)

    def step(*arrays):
        return shards(rows, cols, *arrays)

    return jax.shard_map(step, mesh=mesh, in_specs=in_specs, out_specs=out_specs, check_vma=False)
```

```python
import functools

import jax
import jax.numpy as jnp
from jax import lax
from jax.experimental import pallas as pl
from jax.experimental.pallas import tpu as pltpu
from jax.sharding import PartitionSpec as P

F32, BF16 = jnp.float32, jnp.bfloat16
VMEM_LIMIT = 40 * 1024 * 1024


def sigmoid(values):
    return 0.5 * jnp.tanh(0.5 * values) + 0.5


def normalize(values, gain):
    average = jnp.mean(values, axis=-1, keepdims=True)
    centered = values - average
    spread = jnp.mean(centered * centered, axis=-1, keepdims=True)
    return (centered * lax.rsqrt(spread + 1e-05) * gain).astype(BF16)


def operands_kernel(pair_ref, gain_ref, left_ref, right_ref, sent_ref, turned, sides):
    half, here_k, channels = pair_ref.shape
    width = left_ref.shape[1] // 2
    turned[0] = left_ref[...].astype(F32).T.astype(BF16)
    turned[1] = right_ref[...].astype(F32).T.astype(BF16)
    gain = gain_ref[...]
    for i in range(0, half, 2):
        rows = pair_ref[i : i + 2].reshape(2 * here_k, channels).astype(F32)
        normed = normalize(rows, gain)
        for side in range(2):
            both = lax.dot_general(
                turned[side], normed, (((1,), (1,)), ((), ())), preferred_element_type=F32
            )
            gated = sigmoid(both[:width]) * both[width:]
            sides[side, i] = gated[:, :here_k]
            sides[side, i + 1] = gated[:, here_k:]
    for side in range(2):
        by_channel = jnp.swapaxes(sides[side], 0, 1).astype(BF16)
        chips, _, cols = sent_ref.shape[:3]
        sent_ref[:, 0, :, side] = by_channel.reshape(chips, cols, half, here_k)


def operands(pair, gain, proj_left, proj_right, chips, cols):
    here_i, here_k, channels = pair.shape
    half, width = here_i // 2, proj_left.shape[1] // 2
    whole = lambda array: pl.BlockSpec(array.shape, lambda c: (0,) * array.ndim)
    return pl.pallas_call(
        operands_kernel,
        grid=(2,),
        in_specs=[
            pl.BlockSpec((half, here_k, channels), lambda c: (c, 0, 0)),
            whole(gain),
            whole(proj_left),
            whole(proj_right),
        ],
        out_specs=pl.BlockSpec((chips, 1, cols, 2, half, here_k), lambda c: (0, c, 0, 0, 0, 0)),
        out_shape=jax.ShapeDtypeStruct((chips, 2, cols, 2, half, here_k), BF16),
        scratch_shapes=[
            pltpu.VMEM((2, 2 * width, channels), BF16),
            pltpu.VMEM((2, half, width, here_k), F32),
        ],
        compiler_params=pltpu.CompilerParams(vmem_limit_bytes=VMEM_LIMIT),
        name="operands",
    )(pair, gain, proj_left, proj_right)


def triangle_kernel(core_ref, got_ref, other_ref, product_ref, left, right):
    rows, cols, _, half, here_k = got_ref.shape
    core = core_ref[0]
    for s in range(cols):
        span = pl.ds(s * here_k, here_k)
        left[:, span] = got_ref[:, s, 0].reshape(rows * half, here_k)
        right[:, core, :, span] = got_ref[:, s, 1]
        right[:, 1 - core, :, span] = other_ref[:, s]
    each = rows // cols
    for s in range(0, cols, 2):
        part = right[s * each : (s + 2) * each].reshape(2 * here_k, cols * here_k)
        total = lax.dot_general(
            left[...], part, (((1,), (1,)), ((), ())), preferred_element_type=F32
        ).astype(BF16)
        product_ref[:, s] = total[:, :here_k].reshape(rows, half, here_k)
        product_ref[:, s + 1] = total[:, here_k:].reshape(rows, half, here_k)


def triangle(core, got, other):
    rows, cols, _, half, here_k = got.shape
    vmem = pl.BlockSpec(memory_space=pltpu.VMEM)
    return pl.pallas_call(
        triangle_kernel,
        in_specs=[pl.BlockSpec(memory_space=pltpu.SMEM), vmem, vmem],
        out_specs=vmem,
        out_shape=jax.ShapeDtypeStruct((rows, cols, half, here_k), BF16),
        scratch_shapes=[
            pltpu.VMEM((rows * half, cols * here_k), BF16),
            pltpu.VMEM((rows, 2, half, cols * here_k), BF16),
        ],
        compiler_params=pltpu.CompilerParams(vmem_limit_bytes=VMEM_LIMIT),
        name="triangle",
    )(core, got, other)


def gate_kernel(pair_ref, gain_ref, weight_ref, gate_ref):
    some, here_k, channels = pair_ref.shape
    rows = pair_ref[...].reshape(some * here_k, channels).astype(F32)
    normed = normalize(rows, gain_ref[...])
    gate = sigmoid(jnp.dot(normed, weight_ref[...], preferred_element_type=F32))
    gate_ref[...] = gate.reshape(gate_ref.shape)


def gates(pair, gain, weight):
    here_i, here_k, channels = pair.shape
    some = here_i // 4
    block = pl.BlockSpec((some, here_k, channels), lambda i: (i, 0, 0))
    return pl.pallas_call(
        gate_kernel,
        grid=(4,),
        in_specs=[
            block,
            pl.BlockSpec(gain.shape, lambda i: (0, 0)),
            pl.BlockSpec(weight.shape, lambda i: (0, 0)),
        ],
        out_specs=block,
        out_shape=jax.ShapeDtypeStruct(pair.shape, F32),
        compiler_params=pltpu.CompilerParams(vmem_limit_bytes=VMEM_LIMIT),
        cost_estimate=pl.CostEstimate(
            flops=2 * pair.size * channels, bytes_accessed=6 * pair.size, transcendentals=pair.size
        ),
        name="gates",
    )(pair, gain, weight)


def update_kernel(back_ref, gain_ref, weight_ref, gate_ref, update_ref):
    chips, _, cols, half, here_k = back_ref.shape
    width = chips * cols
    product = back_ref[...].reshape(width, half, here_k).astype(F32)
    average = jnp.mean(product, axis=0, keepdims=True)
    centered = product - average
    spread = jnp.mean(centered * centered, axis=0, keepdims=True)
    normed = centered * lax.rsqrt(spread + 1e-05)
    normed = (jnp.swapaxes(normed, 0, 1) * gain_ref[...]).astype(BF16)
    for i in range(half):
        projected = lax.dot_general(
            normed[i], weight_ref[...], (((0,), (0,)), ((), ())), preferred_element_type=F32
        )
        update_ref[i] = (gate_ref[i] * projected).astype(BF16)


def updates(back, gain, weight, gate):
    chips, _, cols, half, here_k = back.shape
    here_i, _, channels = gate.shape
    block = pl.BlockSpec((half, here_k, channels), lambda c: (c, 0, 0))
    return pl.pallas_call(
        update_kernel,
        grid=(2,),
        in_specs=[
            pl.BlockSpec((chips, 1, cols, half, here_k), lambda c: (0, c, 0, 0, 0)),
            pl.BlockSpec(gain.shape, lambda c: (0, 0)),
            pl.BlockSpec(weight.shape, lambda c: (0, 0)),
            block,
        ],
        out_specs=block,
        out_shape=jax.ShapeDtypeStruct((here_i, here_k, channels), BF16),
        compiler_params=pltpu.CompilerParams(vmem_limit_bytes=VMEM_LIMIT),
        name="updates",
    )(back, gain, weight, gate)


def shards(rows, cols, pair, ln_in_gain, proj_left, proj_right, gate_weight, ln_out_gain, out_weight):
    width = out_weight.shape[0]
    here_i, here_k = pair.shape[0], pair.shape[1]
    half, chips = here_i // 2, rows // 2
    both = ("row", "col")
    exchange = functools.partial(
        lax.all_to_all, axis_name=both, split_axis=0, concat_axis=0, tiled=True
    )
    gain = ln_in_gain.reshape(1, -1)
    sent = operands(pair, gain, proj_left, proj_right, chips, cols)
    got = exchange(sent.reshape(rows * cols, 2, half, here_k))
    got = got.reshape(rows, cols, 2, half, here_k)
    other = lax.ppermute(got[:, :, 1], "row", [(r, r ^ 1) for r in range(rows)])
    core = lax.rem(lax.axis_index("row"), 2).reshape(1)
    product = triangle(core, got, other)
    back = exchange(product.reshape(rows * cols, half, here_k))
    gate = gates(pair, gain, gate_weight)
    return updates(
        back.reshape(chips, 2, cols, half, here_k), ln_out_gain.reshape(width, 1), out_weight, gate
    )


def solution(mesh):
    rows, cols = mesh.shape["row"], mesh.shape["col"]
    in_specs = (P("row", "col", None), P(), P(), P(), P(), P(), P())
    out_specs = P("row", "col", None)
    step = functools.partial(shards, rows, cols)
    return jax.shard_map(step, mesh=mesh, in_specs=in_specs, out_specs=out_specs, check_vma=False)
```

```python
import functools

import jax
import jax.numpy as jnp
from jax import lax
from jax.experimental import pallas as pl
from jax.experimental.pallas import tpu as pltpu
from jax.sharding import PartitionSpec as P

F32, BF16 = jnp.float32, jnp.bfloat16
VMEM_LIMIT = 40 * 1024 * 1024


def sigmoid(values):
    return 0.5 * jnp.tanh(0.5 * values) + 0.5


def normalize(values, gain):
    average = jnp.mean(values, axis=-1, keepdims=True)
    centered = values - average
    spread = jnp.mean(centered * centered, axis=-1, keepdims=True)
    return (centered * lax.rsqrt(spread + 1e-05) * gain).astype(BF16)


PARTS = 4


def operands_kernel(
    pair_hbm, gain_hbm, left_hbm, right_hbm, sent_ref, pair_ref, gain_ref, weights, turned, sides, arrived
):
    here_i, here_k, channels = pair_ref.shape
    chips, cores, cols, _, half, _ = sent_ref.shape
    wide = left_hbm.shape[1]
    width, part = wide // 2, here_i // PARTS
    pieces = [
        pltpu.make_async_copy(
            pair_hbm.at[pl.ds(p * part, part)], pair_ref.at[pl.ds(p * part, part)], arrived.at[p]
        )
        for p in range(PARTS)
    ]
    small = [
        pltpu.make_async_copy(left_hbm, weights.at[0], arrived.at[PARTS]),
        pltpu.make_async_copy(right_hbm, weights.at[1], arrived.at[PARTS + 1]),
        pltpu.make_async_copy(gain_hbm, gain_ref, arrived.at[PARTS + 2]),
    ]
    for copy in pieces[:1] + small + pieces[1:]:
        copy.start()
    for copy in small:
        copy.wait()
    for side in range(2):
        turned[side * wide : (side + 1) * wide] = weights[side].astype(F32).T.astype(BF16)
    gain = gain_ref[...]
    for core in range(cores):
        for i in range(0, half, 2):
            row = core * half + i
            if row % part == 0:
                pieces[row // part].wait()
            rows = pair_ref[row : row + 2].reshape(2 * here_k, channels).astype(F32)
            normed = normalize(rows, gain)
            both = lax.dot_general(
                turned[...], normed, (((1,), (1,)), ((), ())), preferred_element_type=F32
            )
            for side in range(2):
                one = both[side * wide : (side + 1) * wide]
                gated = sigmoid(one[:width]) * one[width:]
                sides[core, side, i] = gated[:, :here_k]
                sides[core, side, i + 1] = gated[:, here_k:]
        for side in range(2):
            by_channel = jnp.swapaxes(sides[core, side], 0, 1).astype(BF16)
            sent_ref[:, core, :, side] = by_channel.reshape(chips, cols, half, here_k)


def operands(pair, gain, proj_left, proj_right, chips, cols):
    here_i, here_k, channels = pair.shape
    half, wide = here_i // 2, proj_left.shape[1]
    hbm = pl.BlockSpec(memory_space=pltpu.HBM)
    arrays = [
        pltpu.with_memory_space_constraint(array, pltpu.HBM)
        for array in (pair, gain, proj_left, proj_right)
    ]
    return pl.pallas_call(
        operands_kernel,
        in_specs=[hbm] * 4,
        out_specs=pl.BlockSpec(memory_space=pltpu.VMEM),
        out_shape=jax.ShapeDtypeStruct((chips, 2, cols, 2, half, here_k), BF16),
        scratch_shapes=[
            pltpu.VMEM(pair.shape, BF16),
            pltpu.VMEM(gain.shape, F32),
            pltpu.VMEM((2, channels, wide), BF16),
            pltpu.VMEM((2 * wide, channels), BF16),
            pltpu.VMEM((2, 2, half, wide // 2, here_k), F32),
            pltpu.SemaphoreType.DMA((PARTS + 3,)),
        ],
        compiler_params=pltpu.CompilerParams(vmem_limit_bytes=VMEM_LIMIT),
        name="operands",
    )(*arrays)


def split_kernel(got_ref, right_ref):
    right_ref[...] = got_ref[:, :, 1]


def split(got):
    rows, cols, _, half, here_k = got.shape
    vmem = pl.BlockSpec(memory_space=pltpu.VMEM)
    return pl.pallas_call(
        split_kernel,
        in_specs=[vmem],
        out_specs=vmem,
        out_shape=jax.ShapeDtypeStruct((rows, cols, half, here_k), BF16),
        compiler_params=pltpu.CompilerParams(vmem_limit_bytes=VMEM_LIMIT),
        name="split",
    )(got)


def own_kernel(got_ref, left_ref, own_ref, right):
    rows, cols, _, half, here_k = got_ref.shape
    for s in range(cols):
        span = pl.ds(s * here_k, here_k)
        left_ref[:, span] = got_ref[:, s, 0].reshape(rows * half, here_k)
        right[:, span] = got_ref[:, s, 1].reshape(rows * half, here_k)
    step = 2 * here_k
    for j in range(0, rows * half, step):
        own_ref[:, j : j + step] = lax.dot_general(
            left_ref[...], right[j : j + step], (((1,), (1,)), ((), ())), preferred_element_type=F32
        ).astype(BF16)


def own_part(got):
    rows, cols, _, half, here_k = got.shape
    tall, deep = rows * half, cols * here_k
    vmem = pl.BlockSpec(memory_space=pltpu.VMEM)
    return pl.pallas_call(
        own_kernel,
        in_specs=[vmem],
        out_specs=[vmem, vmem],
        out_shape=[
            jax.ShapeDtypeStruct((tall, deep), BF16),
            jax.ShapeDtypeStruct((tall, tall), BF16),
        ],
        scratch_shapes=[pltpu.VMEM((tall, deep), BF16)],
        compiler_params=pltpu.CompilerParams(vmem_limit_bytes=VMEM_LIMIT),
        cost_estimate=pl.CostEstimate(
            flops=2 * tall * tall * deep, bytes_accessed=8 * tall * deep, transcendentals=0
        ),
        name="own_part",
    )(got)


def merge_kernel(left_ref, own_ref, other_ref, product_ref, right):
    rows, cols, half, here_k = other_ref.shape
    each = rows // cols * half
    for s in range(cols):
        span = pl.ds(s * here_k, here_k)
        block = other_ref[:, s].reshape(cols // 2, 2, each, here_k)
        right[:, 1, :, span] = block[:, 0]
        right[:, 0, :, span] = block[:, 1]
    first = lax.broadcasted_iota(jnp.int32, (1, here_k), 1) < each
    for pair in range(0, cols // 2, 2):
        part = right[pair : pair + 2].reshape(2 * here_k, cols * here_k)
        total = lax.dot_general(
            left_ref[...], part, (((1,), (1,)), ((), ())), preferred_element_type=F32
        )
        for p in range(2):
            span = pl.ds((pair + p) * here_k, here_k)
            own = own_ref[:, span].astype(F32)
            other = total[:, p * here_k : (p + 1) * here_k]
            even = jnp.where(first, own, other).astype(BF16)
            odd = jnp.where(first, other, own).astype(BF16)
            product_ref[:, 2 * (pair + p)] = even.reshape(rows, half, here_k)
            product_ref[:, 2 * (pair + p) + 1] = odd.reshape(rows, half, here_k)


def merge(left, own, other):
    rows, cols, half, here_k = other.shape
    vmem = pl.BlockSpec(memory_space=pltpu.VMEM)
    return pl.pallas_call(
        merge_kernel,
        in_specs=[vmem, vmem, vmem],
        out_specs=vmem,
        out_shape=jax.ShapeDtypeStruct(other.shape, BF16),
        scratch_shapes=[
            pltpu.VMEM((cols // 2, 2, rows // cols * half, cols * here_k), BF16),
        ],
        compiler_params=pltpu.CompilerParams(vmem_limit_bytes=VMEM_LIMIT),
        name="merge",
    )(left, own, other)


def gate_kernel(pair_ref, gain_ref, weight_ref, gate_ref):
    some, here_k, channels = pair_ref.shape
    rows = pair_ref[...].reshape(some * here_k, channels).astype(F32)
    normed = normalize(rows, gain_ref[...])
    gate = sigmoid(jnp.dot(normed, weight_ref[...], preferred_element_type=F32))
    gate_ref[...] = gate.reshape(gate_ref.shape)


def gates(pair, gain, weight):
    here_i, here_k, channels = pair.shape
    some = here_i // 4
    block = pl.BlockSpec((some, here_k, channels), lambda i: (i, 0, 0))
    return pl.pallas_call(
        gate_kernel,
        grid=(4,),
        in_specs=[
            block,
            pl.BlockSpec(gain.shape, lambda i: (0, 0)),
            pl.BlockSpec(weight.shape, lambda i: (0, 0)),
        ],
        out_specs=block,
        out_shape=jax.ShapeDtypeStruct(pair.shape, F32),
        compiler_params=pltpu.CompilerParams(vmem_limit_bytes=VMEM_LIMIT),
        cost_estimate=pl.CostEstimate(
            flops=2 * pair.size * channels, bytes_accessed=6 * pair.size, transcendentals=pair.size
        ),
        name="gates",
    )(pair, gain, weight)


def update_kernel(
    odd_ref, back_hbm, gain_ref, weight_ref, gate_ref, update_hbm, back_ref, update_ref, arrived, left
):
    chips, cores, cols, half, here_k = back_ref.shape
    width, each = chips * cols, gate_ref.shape[1]
    channels = gate_ref.shape[4]
    odd = odd_ref[0]
    incoming = [
        pltpu.make_async_copy(back_hbm.at[:, c], back_ref.at[:, c], arrived.at[c])
        for c in range(cores)
    ]
    for copy in incoming:
        copy.start()
    gain = jnp.broadcast_to(gain_ref[...], (here_k, width)).T
    outgoing = []
    for c in range(cores):
        incoming[c].wait()
        product = back_ref[:, c].reshape(width, half, here_k).astype(F32)
        average = jnp.mean(product, axis=0, keepdims=True)
        centered = product - average
        spread = jnp.mean(centered * centered, axis=0, keepdims=True)
        normed = centered * lax.rsqrt(spread + 1e-05)
        normed = (jnp.swapaxes(normed, 0, 1) * gain).astype(BF16)
        first = (c + odd) % 2
        for i in range(half):
            row = c * half + i
            projected = lax.dot_general(
                normed[i], weight_ref[...], (((0,), (0,)), ((), ())), preferred_element_type=F32
            ).reshape(2, each, half, channels)
            update_ref[row, :, first] = (gate_ref[row, :, first] * projected[0]).astype(BF16)
            second = 1 - first
            update_ref[row, :, second] = (gate_ref[row, :, second] * projected[1]).astype(BF16)
            if (i + 1) % 4 == 0:
                span = pl.ds(row - 3, 4)
                copy = pltpu.make_async_copy(
                    update_ref.at[span], update_hbm.at[span], left.at[len(outgoing)]
                )
                copy.start()
                outgoing.append(copy)
    for copy in outgoing:
        copy.wait()


def updates(odd, back, gain, weight, gate):
    chips, _, cols, half, here_k = back.shape
    here_i, _, channels = gate.shape
    blocked = (here_i, here_k // (2 * half), 2, half, channels)
    vmem, hbm = pl.BlockSpec(memory_space=pltpu.VMEM), pl.BlockSpec(memory_space=pltpu.HBM)
    update = pl.pallas_call(
        update_kernel,
        in_specs=[pl.BlockSpec(memory_space=pltpu.SMEM), hbm, vmem, vmem, vmem],
        out_specs=hbm,
        out_shape=jax.ShapeDtypeStruct(blocked, BF16),
        scratch_shapes=[
            pltpu.VMEM(back.shape, BF16),
            pltpu.VMEM(blocked, BF16),
            pltpu.SemaphoreType.DMA((2,)),
            pltpu.SemaphoreType.DMA((here_i // 4,)),
        ],
        compiler_params=pltpu.CompilerParams(vmem_limit_bytes=VMEM_LIMIT),
        name="updates",
    )(odd, back, gain, weight, gate.reshape(blocked))
    return update.reshape(gate.shape)


def shards(rows, cols, pair, ln_in_gain, proj_left, proj_right, gate_weight, ln_out_gain, out_weight):
    width = out_weight.shape[0]
    here_i, here_k = pair.shape[0], pair.shape[1]
    half, chips = here_i // 2, rows // 2
    both = ("row", "col")
    exchange = functools.partial(
        lax.all_to_all, axis_name=both, split_axis=0, concat_axis=0, tiled=True
    )
    gain = ln_in_gain.reshape(1, -1)
    sent = operands(pair, gain, proj_left, proj_right, chips, cols)
    got = exchange(sent.reshape(rows * cols, 2, half, here_k))
    got = got.reshape(rows, cols, 2, half, here_k)
    other = lax.ppermute(split(got), "row", [(r, r ^ 1) for r in range(rows)])
    left, own = own_part(got)
    product = merge(left, own, other)
    product, late_pair = lax.optimization_barrier((product, pair))
    back = exchange(product.reshape(rows * cols, half, here_k))
    gate = gates(late_pair, gain, gate_weight)
    odd = lax.rem(lax.axis_index("col"), 2).reshape(1)
    return updates(
        odd, back.reshape(chips, 2, cols, half, here_k), ln_out_gain.reshape(1, width), out_weight, gate
    )


def solution(mesh):
    rows, cols = mesh.shape["row"], mesh.shape["col"]
    in_specs = (P("row", "col", None), P(), P(), P(), P(), P(), P())
    out_specs = P("row", "col", None)
    step = functools.partial(shards, rows, cols)
    return jax.shard_map(step, mesh=mesh, in_specs=in_specs, out_specs=out_specs, check_vma=False)
```

```python
import functools

import jax
import jax.numpy as jnp
from jax import lax
from jax.experimental import pallas as pl
from jax.experimental.pallas import tpu as pltpu
from jax.sharding import PartitionSpec as P

F32, BF16 = jnp.float32, jnp.bfloat16
VMEM_LIMIT = 40 * 1024 * 1024


def sigmoid(values):
    return 0.5 * jnp.tanh(0.5 * values) + 0.5


def normalize(values, gain):
    average = jnp.mean(values, axis=-1, keepdims=True)
    centered = values - average
    spread = jnp.mean(centered * centered, axis=-1, keepdims=True)
    return (centered * lax.rsqrt(spread + 1e-05) * gain).astype(BF16)


PARTS = 4


def operands_kernel(
    pair_hbm, gain_hbm, left_hbm, right_hbm, sent_ref, pair_ref, gain_ref, weights, turned, sides, arrived
):
    here_i, here_k, channels = pair_ref.shape
    chips, cores, cols, _, half, _ = sent_ref.shape
    wide = left_hbm.shape[1]
    width, part = wide // 2, here_i // PARTS
    pieces = [
        pltpu.make_async_copy(
            pair_hbm.at[pl.ds(p * part, part)], pair_ref.at[pl.ds(p * part, part)], arrived.at[p]
        )
        for p in range(PARTS)
    ]
    small = [
        pltpu.make_async_copy(left_hbm, weights.at[0], arrived.at[PARTS]),
        pltpu.make_async_copy(right_hbm, weights.at[1], arrived.at[PARTS + 1]),
        pltpu.make_async_copy(gain_hbm, gain_ref, arrived.at[PARTS + 2]),
    ]
    for copy in pieces[:1] + small + pieces[1:]:
        copy.start()
    for copy in small:
        copy.wait()
    for side in range(2):
        turned[side * wide : (side + 1) * wide] = (0.5 * weights[side].astype(F32)).T.astype(BF16)
    gain = gain_ref[...]
    for core in range(cores):
        for i in range(0, half, 2):
            row = core * half + i
            if row % part == 0:
                pieces[row // part].wait()
            rows = pair_ref[row : row + 2].reshape(2 * here_k, channels).astype(F32)
            normed = normalize(rows, gain)
            both = lax.dot_general(
                turned[...], normed, (((1,), (1,)), ((), ())), preferred_element_type=F32
            )
            for side in range(2):
                one = both[side * wide : (side + 1) * wide]
                gated = (jnp.tanh(one[:width]) + 1.0) * one[width:]
                sides[core, side, i] = gated[:, :here_k]
                sides[core, side, i + 1] = gated[:, here_k:]
        for side in range(2):
            by_channel = jnp.swapaxes(sides[core, side], 0, 1).astype(BF16)
            sent_ref[:, core, :, side] = by_channel.reshape(chips, cols, half, here_k)


def operands(pair, gain, proj_left, proj_right, chips, cols):
    here_i, here_k, channels = pair.shape
    half, wide = here_i // 2, proj_left.shape[1]
    hbm = pl.BlockSpec(memory_space=pltpu.HBM)
    arrays = [
        pltpu.with_memory_space_constraint(array, pltpu.HBM)
        for array in (pair, gain, proj_left, proj_right)
    ]
    return pl.pallas_call(
        operands_kernel,
        in_specs=[hbm] * 4,
        out_specs=pl.BlockSpec(memory_space=pltpu.VMEM),
        out_shape=jax.ShapeDtypeStruct((chips, 2, cols, 2, half, here_k), BF16),
        scratch_shapes=[
            pltpu.VMEM(pair.shape, BF16),
            pltpu.VMEM(gain.shape, F32),
            pltpu.VMEM((2, channels, wide), BF16),
            pltpu.VMEM((2 * wide, channels), BF16),
            pltpu.VMEM((2, 2, half, wide // 2, here_k), F32),
            pltpu.SemaphoreType.DMA((PARTS + 3,)),
        ],
        compiler_params=pltpu.CompilerParams(vmem_limit_bytes=VMEM_LIMIT),
        name="operands",
    )(*arrays)


def split_kernel(got_ref, right_ref):
    right_ref[...] = got_ref[:, :, 1]


def split(got):
    rows, cols, _, half, here_k = got.shape
    vmem = pl.BlockSpec(memory_space=pltpu.VMEM)
    return pl.pallas_call(
        split_kernel,
        in_specs=[vmem],
        out_specs=vmem,
        out_shape=jax.ShapeDtypeStruct((rows, cols, half, here_k), BF16),
        compiler_params=pltpu.CompilerParams(vmem_limit_bytes=VMEM_LIMIT),
        name="split",
    )(got)


def own_kernel(got_ref, left_ref, own_ref, right):
    rows, cols, _, half, here_k = got_ref.shape
    for s in range(cols):
        span = pl.ds(s * here_k, here_k)
        left_ref[:, span] = got_ref[:, s, 0].reshape(rows * half, here_k)
        right[:, span] = got_ref[:, s, 1].reshape(rows * half, here_k)
    step = 2 * here_k
    for j in range(0, rows * half, step):
        own_ref[:, j : j + step] = lax.dot_general(
            left_ref[...], right[j : j + step], (((1,), (1,)), ((), ())), preferred_element_type=F32
        ).astype(BF16)


def own_part(got):
    rows, cols, _, half, here_k = got.shape
    tall, deep = rows * half, cols * here_k
    vmem = pl.BlockSpec(memory_space=pltpu.VMEM)
    return pl.pallas_call(
        own_kernel,
        in_specs=[vmem],
        out_specs=[vmem, vmem],
        out_shape=[
            jax.ShapeDtypeStruct((tall, deep), BF16),
            jax.ShapeDtypeStruct((tall, tall), BF16),
        ],
        scratch_shapes=[pltpu.VMEM((tall, deep), BF16)],
        compiler_params=pltpu.CompilerParams(vmem_limit_bytes=VMEM_LIMIT),
        cost_estimate=pl.CostEstimate(
            flops=2 * tall * tall * deep, bytes_accessed=8 * tall * deep, transcendentals=0
        ),
        name="own_part",
    )(got)


def merge_kernel(left_ref, own_ref, other_ref, product_hbm, product_ref, right, left):
    rows, cols, half, here_k = other_ref.shape
    each = rows // cols * half
    for s in range(cols):
        span = pl.ds(s * here_k, here_k)
        block = other_ref[:, s].reshape(cols // 2, 2, each, here_k)
        right[:, 1, :, span] = block[:, 0]
        right[:, 0, :, span] = block[:, 1]
    outgoing = []
    first = lax.broadcasted_iota(jnp.int32, (1, here_k), 1) < each
    for pair in range(0, cols // 2, 2):
        part = right[pair : pair + 2].reshape(2 * here_k, cols * here_k)
        total = lax.dot_general(
            left_ref[...], part, (((1,), (1,)), ((), ())), preferred_element_type=F32
        )
        for p in range(2):
            span = pl.ds((pair + p) * here_k, here_k)
            own = own_ref[:, span].astype(F32)
            other = total[:, p * here_k : (p + 1) * here_k]
            even = jnp.where(first, own, other).astype(BF16)
            odd = jnp.where(first, other, own).astype(BF16)
            product_ref[:, 2 * (pair + p)] = even.reshape(rows, half, here_k)
            product_ref[:, 2 * (pair + p) + 1] = odd.reshape(rows, half, here_k)
            span = pl.ds(2 * (pair + p), 2)
            copy = pltpu.make_async_copy(
                product_ref.at[:, span], product_hbm.at[:, span], left.at[pair + p]
            )
            copy.start()
            outgoing.append(copy)
    for copy in outgoing:
        copy.wait()


def merge(left, own, other):
    rows, cols, half, here_k = other.shape
    vmem = pl.BlockSpec(memory_space=pltpu.VMEM)
    return pl.pallas_call(
        merge_kernel,
        in_specs=[vmem, vmem, vmem],
        out_specs=pl.BlockSpec(memory_space=pltpu.HBM),
        out_shape=jax.ShapeDtypeStruct(other.shape, BF16),
        scratch_shapes=[
            pltpu.VMEM(other.shape, BF16),
            pltpu.VMEM((cols // 2, 2, rows // cols * half, cols * here_k), BF16),
            pltpu.SemaphoreType.DMA((cols // 2,)),
        ],
        compiler_params=pltpu.CompilerParams(vmem_limit_bytes=VMEM_LIMIT),
        name="merge",
    )(left, own, other)


def gate_kernel(pair_ref, gain_ref, weight_ref, gate_ref):
    some, here_k, channels = pair_ref.shape
    rows = pair_ref[...].reshape(some * here_k, channels).astype(F32)
    normed = normalize(rows, gain_ref[...])
    gate = sigmoid(jnp.dot(normed, weight_ref[...], preferred_element_type=F32))
    gate_ref[...] = gate.reshape(gate_ref.shape)


def gates(pair, gain, weight):
    here_i, here_k, channels = pair.shape
    some = here_i // 4
    block = pl.BlockSpec((some, here_k, channels), lambda i: (i, 0, 0))
    return pl.pallas_call(
        gate_kernel,
        grid=(4,),
        in_specs=[
            block,
            pl.BlockSpec(gain.shape, lambda i: (0, 0)),
            pl.BlockSpec(weight.shape, lambda i: (0, 0)),
        ],
        out_specs=block,
        out_shape=jax.ShapeDtypeStruct(pair.shape, F32),
        compiler_params=pltpu.CompilerParams(vmem_limit_bytes=VMEM_LIMIT),
        cost_estimate=pl.CostEstimate(
            flops=2 * pair.size * channels, bytes_accessed=6 * pair.size, transcendentals=pair.size
        ),
        name="gates",
    )(pair, gain, weight)


def update_kernel(
    odd_ref, back_ref, gain_ref, weight_ref, gate_ref, update_hbm, update_ref, left
):
    chips, cores, cols, half, here_k = back_ref.shape
    width, each = chips * cols, gate_ref.shape[1]
    channels = gate_ref.shape[4]
    odd = odd_ref[0]
    gain = jnp.broadcast_to(gain_ref[...], (here_k, width)).T
    outgoing = []
    for c in range(cores):
        product = back_ref[:, c].reshape(width, half, here_k).astype(F32)
        average = jnp.mean(product, axis=0, keepdims=True)
        centered = product - average
        spread = jnp.mean(centered * centered, axis=0, keepdims=True)
        normed = centered * lax.rsqrt(spread + 1e-05)
        normed = (jnp.swapaxes(normed, 0, 1) * gain).astype(BF16)
        first = (c + odd) % 2
        for i in range(half):
            row = c * half + i
            projected = lax.dot_general(
                normed[i], weight_ref[...], (((0,), (0,)), ((), ())), preferred_element_type=F32
            ).reshape(2, each, half, channels)
            update_ref[row, :, first] = (gate_ref[row, :, first] * projected[0]).astype(BF16)
            second = 1 - first
            update_ref[row, :, second] = (gate_ref[row, :, second] * projected[1]).astype(BF16)
            if (i + 1) % 4 == 0:
                span = pl.ds(row - 3, 4)
                copy = pltpu.make_async_copy(
                    update_ref.at[span], update_hbm.at[span], left.at[len(outgoing)]
                )
                copy.start()
                outgoing.append(copy)
    for copy in outgoing:
        copy.wait()


def updates(odd, back, gain, weight, gate):
    chips, _, cols, half, here_k = back.shape
    here_i, _, channels = gate.shape
    blocked = (here_i, here_k // (2 * half), 2, half, channels)
    vmem, hbm = pl.BlockSpec(memory_space=pltpu.VMEM), pl.BlockSpec(memory_space=pltpu.HBM)
    update = pl.pallas_call(
        update_kernel,
        in_specs=[pl.BlockSpec(memory_space=pltpu.SMEM), vmem, vmem, vmem, vmem],
        out_specs=hbm,
        out_shape=jax.ShapeDtypeStruct(blocked, BF16),
        scratch_shapes=[
            pltpu.VMEM(blocked, BF16),
            pltpu.SemaphoreType.DMA((here_i // 4,)),
        ],
        compiler_params=pltpu.CompilerParams(vmem_limit_bytes=VMEM_LIMIT),
        name="updates",
    )(odd, back, gain, weight, gate.reshape(blocked))
    return update.reshape(gate.shape)


def shards(rows, cols, pair, ln_in_gain, proj_left, proj_right, gate_weight, ln_out_gain, out_weight):
    width = out_weight.shape[0]
    here_i, here_k = pair.shape[0], pair.shape[1]
    half, chips = here_i // 2, rows // 2
    both = ("row", "col")
    exchange = functools.partial(
        lax.all_to_all, axis_name=both, split_axis=0, concat_axis=0, tiled=True
    )
    gain = ln_in_gain.reshape(1, -1)
    sent = operands(pair, gain, proj_left, proj_right, chips, cols)
    got = exchange(sent.reshape(rows * cols, 2, half, here_k))
    got = got.reshape(rows, cols, 2, half, here_k)
    other = lax.ppermute(split(got), "row", [(r, r ^ 1) for r in range(rows)])
    left, own = own_part(got)
    product = merge(left, own, other)
    product, late_pair = lax.optimization_barrier((product, pair))
    back = exchange(product.reshape(rows * cols, half, here_k))
    gate = gates(late_pair, gain, gate_weight)
    odd = lax.rem(lax.axis_index("col"), 2).reshape(1)
    return updates(
        odd, back.reshape(chips, 2, cols, half, here_k), ln_out_gain.reshape(1, width), out_weight, gate
    )


def solution(mesh):
    rows, cols = mesh.shape["row"], mesh.shape["col"]
    in_specs = (P("row", "col", None), P(), P(), P(), P(), P(), P())
    out_specs = P("row", "col", None)
    step = functools.partial(shards, rows, cols)
    return jax.shard_map(step, mesh=mesh, in_specs=in_specs, out_specs=out_specs, check_vma=False)
```

```python
import functools

import jax
import jax.numpy as jnp
from jax import lax
from jax.experimental import pallas as pl
from jax.experimental.pallas import tpu as pltpu
from jax.sharding import PartitionSpec as P

F32, BF16 = jnp.float32, jnp.bfloat16
VMEM_LIMIT = 40 * 1024 * 1024


def sigmoid(values):
    return 0.5 * jnp.tanh(0.5 * values) + 0.5


def normalize(values, gain):
    average = jnp.mean(values, axis=-1, keepdims=True)
    centered = values - average
    spread = jnp.mean(centered * centered, axis=-1, keepdims=True)
    return (centered * lax.rsqrt(spread + 1e-05) * gain).astype(BF16)


PARTS = 4
STRIP = 16


def operands_kernel(
    pair_hbm, gain_hbm, left_hbm, right_hbm, sent_ref, pair_ref, gain_ref, weights, turned, sides, arrived
):
    here_i, here_k, channels = pair_ref.shape
    chips, cols = sent_ref.shape[:2]
    wide = left_hbm.shape[1]
    width, part = wide // 2, here_i // PARTS
    pieces = [
        pltpu.make_async_copy(
            pair_hbm.at[pl.ds(p * part, part)], pair_ref.at[pl.ds(p * part, part)], arrived.at[p]
        )
        for p in range(PARTS)
    ]
    small = [
        pltpu.make_async_copy(left_hbm, weights.at[0], arrived.at[PARTS]),
        pltpu.make_async_copy(right_hbm, weights.at[1], arrived.at[PARTS + 1]),
        pltpu.make_async_copy(gain_hbm, gain_ref, arrived.at[PARTS + 2]),
    ]
    for copy in pieces[:1] + small + pieces[1:]:
        copy.start()
    for copy in small:
        copy.wait()
    for side in range(2):
        turned[side * wide : (side + 1) * wide] = (0.5 * weights[side].astype(F32)).T.astype(BF16)
    gain = gain_ref[...]
    for start in range(0, here_i, STRIP):
        strip = start // STRIP
        for i in range(0, STRIP, 2):
            row = start + i
            if row % part == 0:
                pieces[row // part].wait()
            rows = pair_ref[row : row + 2].reshape(2 * here_k, channels).astype(F32)
            normed = normalize(rows, gain)
            both = lax.dot_general(
                turned[...], normed, (((1,), (1,)), ((), ())), preferred_element_type=F32
            )
            for side in range(2):
                one = both[side * wide : (side + 1) * wide]
                gated = (jnp.tanh(one[:width]) + 1.0) * one[width:]
                sides[strip, side, i] = gated[:, :here_k]
                sides[strip, side, i + 1] = gated[:, here_k:]
        for side in range(2):
            by_channel = jnp.swapaxes(sides[strip, side], 0, 1).astype(BF16)
            sent_ref[:, :, side, start : start + STRIP] = by_channel.reshape(
                chips, cols, STRIP, here_k
            )


def operands(pair, gain, proj_left, proj_right, chips, cols):
    here_i, here_k, channels = pair.shape
    wide = proj_left.shape[1]
    hbm = pl.BlockSpec(memory_space=pltpu.HBM)
    arrays = [
        pltpu.with_memory_space_constraint(array, pltpu.HBM)
        for array in (pair, gain, proj_left, proj_right)
    ]
    return pl.pallas_call(
        operands_kernel,
        in_specs=[hbm] * 4,
        out_specs=pl.BlockSpec(memory_space=pltpu.VMEM),
        out_shape=jax.ShapeDtypeStruct((chips, cols, 2, here_i, here_k), BF16),
        scratch_shapes=[
            pltpu.VMEM(pair.shape, BF16),
            pltpu.VMEM(gain.shape, F32),
            pltpu.VMEM((2, channels, wide), BF16),
            pltpu.VMEM((2 * wide, channels), BF16),
            pltpu.VMEM((here_i // STRIP, 2, STRIP, wide // 2, here_k), F32),
            pltpu.SemaphoreType.DMA((PARTS + 3,)),
        ],
        compiler_params=pltpu.CompilerParams(vmem_limit_bytes=VMEM_LIMIT),
        name="operands",
    )(*arrays)


def split_kernel(got_ref, right_ref):
    right_ref[...] = got_ref[:, :, 1]


def split(got):
    rows, cols, _, half, here_k = got.shape
    vmem = pl.BlockSpec(memory_space=pltpu.VMEM)
    return pl.pallas_call(
        split_kernel,
        in_specs=[vmem],
        out_specs=vmem,
        out_shape=jax.ShapeDtypeStruct((rows, cols, half, here_k), BF16),
        compiler_params=pltpu.CompilerParams(vmem_limit_bytes=VMEM_LIMIT),
        name="split",
    )(got)


def own_kernel(got_ref, left_ref, own_ref, right):
    rows, cols, _, half, here_k = got_ref.shape
    for s in range(cols):
        span = pl.ds(s * here_k, here_k)
        left_ref[:, span] = got_ref[:, s, 0].reshape(rows * half, here_k)
        right[:, span] = got_ref[:, s, 1].reshape(rows * half, here_k)
    step = 2 * here_k
    for j in range(0, rows * half, step):
        own_ref[:, j : j + step] = lax.dot_general(
            left_ref[...], right[j : j + step], (((1,), (1,)), ((), ())), preferred_element_type=F32
        ).astype(BF16)


def own_part(got):
    rows, cols, _, half, here_k = got.shape
    tall, deep = rows * half, cols * here_k
    vmem = pl.BlockSpec(memory_space=pltpu.VMEM)
    return pl.pallas_call(
        own_kernel,
        in_specs=[vmem],
        out_specs=[vmem, vmem],
        out_shape=[
            jax.ShapeDtypeStruct((tall, deep), BF16),
            jax.ShapeDtypeStruct((tall, tall), BF16),
        ],
        scratch_shapes=[pltpu.VMEM((tall, deep), BF16)],
        compiler_params=pltpu.CompilerParams(vmem_limit_bytes=VMEM_LIMIT),
        cost_estimate=pl.CostEstimate(
            flops=2 * tall * tall * deep, bytes_accessed=8 * tall * deep, transcendentals=0
        ),
        name="own_part",
    )(got)


def merge_kernel(left_ref, own_ref, other_ref, product_hbm, product_ref, right, left):
    rows, cols, half, here_k = other_ref.shape
    each = rows // cols * half
    for s in range(cols):
        span = pl.ds(s * here_k, here_k)
        block = other_ref[:, s].reshape(cols // 2, 2, each, here_k)
        right[:, 1, :, span] = block[:, 0]
        right[:, 0, :, span] = block[:, 1]
    outgoing = []
    first = lax.broadcasted_iota(jnp.int32, (1, here_k), 1) < each
    for pair in range(0, cols // 2, 2):
        part = right[pair : pair + 2].reshape(2 * here_k, cols * here_k)
        total = lax.dot_general(
            left_ref[...], part, (((1,), (1,)), ((), ())), preferred_element_type=F32
        )
        for p in range(2):
            span = pl.ds((pair + p) * here_k, here_k)
            own = own_ref[:, span].astype(F32)
            other = total[:, p * here_k : (p + 1) * here_k]
            even = jnp.where(first, own, other).astype(BF16)
            odd = jnp.where(first, other, own).astype(BF16)
            product_ref[:, 2 * (pair + p)] = even.reshape(rows, half, here_k)
            product_ref[:, 2 * (pair + p) + 1] = odd.reshape(rows, half, here_k)
            span = pl.ds(2 * (pair + p), 2)
            copy = pltpu.make_async_copy(
                product_ref.at[:, span], product_hbm.at[:, span], left.at[pair + p]
            )
            copy.start()
            outgoing.append(copy)
    for copy in outgoing:
        copy.wait()


def merge(left, own, other):
    rows, cols, half, here_k = other.shape
    vmem = pl.BlockSpec(memory_space=pltpu.VMEM)
    return pl.pallas_call(
        merge_kernel,
        in_specs=[vmem, vmem, vmem],
        out_specs=pl.BlockSpec(memory_space=pltpu.HBM),
        out_shape=jax.ShapeDtypeStruct(other.shape, BF16),
        scratch_shapes=[
            pltpu.VMEM(other.shape, BF16),
            pltpu.VMEM((cols // 2, 2, rows // cols * half, cols * here_k), BF16),
            pltpu.SemaphoreType.DMA((cols // 2,)),
        ],
        compiler_params=pltpu.CompilerParams(vmem_limit_bytes=VMEM_LIMIT),
        name="merge",
    )(left, own, other)


def gate_kernel(pair_ref, gain_ref, weight_ref, gate_ref):
    some, here_k, channels = pair_ref.shape
    rows = pair_ref[...].reshape(some * here_k, channels).astype(F32)
    normed = normalize(rows, gain_ref[...])
    gate = sigmoid(jnp.dot(normed, weight_ref[...], preferred_element_type=F32))
    gate_ref[...] = gate.reshape(gate_ref.shape)


def gates(pair, gain, weight):
    here_i, here_k, channels = pair.shape
    some = here_i // 4
    block = pl.BlockSpec((some, here_k, channels), lambda i: (i, 0, 0))
    return pl.pallas_call(
        gate_kernel,
        grid=(4,),
        in_specs=[
            block,
            pl.BlockSpec(gain.shape, lambda i: (0, 0)),
            pl.BlockSpec(weight.shape, lambda i: (0, 0)),
        ],
        out_specs=block,
        out_shape=jax.ShapeDtypeStruct(pair.shape, F32),
        compiler_params=pltpu.CompilerParams(vmem_limit_bytes=VMEM_LIMIT),
        cost_estimate=pl.CostEstimate(
            flops=2 * pair.size * channels, bytes_accessed=6 * pair.size, transcendentals=pair.size
        ),
        name="gates",
    )(pair, gain, weight)


def update_kernel(
    first_ref, back_ref, gain_ref, weight_ref, gate_ref, update_hbm, update_ref, left
):
    chips, cols, here_i, here_k = back_ref.shape
    width = chips * cols
    _, each, _, run, channels = gate_ref.shape
    first = first_ref[0]
    second = 1 - first
    gain = jnp.broadcast_to(gain_ref[...], (here_k, width)).T
    outgoing = []
    for start in range(0, here_i, STRIP):
        product = back_ref[:, :, start : start + STRIP].reshape(width, STRIP, here_k).astype(F32)
        average = jnp.mean(product, axis=0, keepdims=True)
        centered = product - average
        spread = jnp.mean(centered * centered, axis=0, keepdims=True)
        normed = centered * lax.rsqrt(spread + 1e-05)
        normed = (jnp.swapaxes(normed, 0, 1) * gain).astype(BF16)
        for i in range(STRIP):
            row = start + i
            projected = lax.dot_general(
                normed[i], weight_ref[...], (((0,), (0,)), ((), ())), preferred_element_type=F32
            ).reshape(2, each, run, channels)
            update_ref[row, :, first] = (gate_ref[row, :, first] * projected[0]).astype(BF16)
            update_ref[row, :, second] = (gate_ref[row, :, second] * projected[1]).astype(BF16)
            if (i + 1) % 4 == 0:
                span = pl.ds(row - 3, 4)
                copy = pltpu.make_async_copy(
                    update_ref.at[span], update_hbm.at[span], left.at[len(outgoing)]
                )
                copy.start()
                outgoing.append(copy)
    for copy in outgoing:
        copy.wait()


def updates(first, back, gain, weight, gate):
    here_i, here_k, channels = gate.shape
    blocked = (here_i, here_k // (2 * here_i), 2, here_i, channels)
    vmem, hbm = pl.BlockSpec(memory_space=pltpu.VMEM), pl.BlockSpec(memory_space=pltpu.HBM)
    update = pl.pallas_call(
        update_kernel,
        in_specs=[pl.BlockSpec(memory_space=pltpu.SMEM), vmem, vmem, vmem, vmem],
        out_specs=hbm,
        out_shape=jax.ShapeDtypeStruct(blocked, BF16),
        scratch_shapes=[
            pltpu.VMEM(blocked, BF16),
            pltpu.SemaphoreType.DMA((here_i // 4,)),
        ],
        compiler_params=pltpu.CompilerParams(vmem_limit_bytes=VMEM_LIMIT),
        name="updates",
    )(first, back, gain, weight, gate.reshape(blocked))
    return update.reshape(gate.shape)


def shards(chips, cols, pair, ln_in_gain, proj_left, proj_right, gate_weight, ln_out_gain, out_weight):
    width = out_weight.shape[0]
    here_i, here_k = pair.shape[0], pair.shape[1]
    exchange = functools.partial(
        lax.all_to_all, axis_name=("chip", "col"), split_axis=0, concat_axis=0, tiled=True
    )
    gain = ln_in_gain.reshape(1, -1)
    sent = operands(pair, gain, proj_left, proj_right, chips, cols)
    got = exchange(sent.reshape(chips * cols, 2, here_i, here_k))
    got = got.reshape(chips, cols, 2, here_i, here_k)
    other = lax.ppermute(split(got), "core", [(0, 1), (1, 0)])
    left, own = own_part(got)
    product = merge(left, own, other)
    product, late_pair = lax.optimization_barrier((product, pair))
    back = exchange(product.reshape(chips * cols, here_i, here_k))
    gate = gates(late_pair, gain, gate_weight)
    first = lax.rem(lax.axis_index("core") + lax.axis_index("col"), 2).reshape(1)
    return updates(
        first, back.reshape(chips, cols, here_i, here_k), ln_out_gain.reshape(1, width), out_weight, gate
    )


def solution(mesh):
    rows, cols = mesh.shape["row"], mesh.shape["col"]
    chips = rows // 2
    by_core = jax.sharding.Mesh(mesh.devices.reshape(chips, 2, cols), ("chip", "core", "col"))
    cells = P(("chip", "core"), "col", None)
    step = functools.partial(shards, chips, cols)
    return jax.shard_map(
        step, mesh=by_core, in_specs=(cells,) + (P(),) * 6, out_specs=cells, check_vma=False
    )
```

```python
import functools

import jax
import jax.numpy as jnp
from jax import lax
from jax.experimental import pallas as pl
from jax.experimental.pallas import tpu as pltpu
from jax.sharding import PartitionSpec as P

F32, BF16 = jnp.float32, jnp.bfloat16
VMEM_LIMIT = 40 * 1024 * 1024


def normalize(values, gain):
    average = jnp.mean(values, axis=-1, keepdims=True)
    centered = values - average
    spread = jnp.mean(centered * centered, axis=-1, keepdims=True)
    return (centered * lax.rsqrt(spread + 1e-05) * gain).astype(BF16)


PARTS = 4
STRIP = 16


def operands_kernel(
    pair_hbm, gain_hbm, left_hbm, right_hbm, sent_ref, pair_ref, gain_ref, weights, turned, sides, arrived
):
    here_i, here_k, channels = pair_ref.shape
    chips, cols = sent_ref.shape[:2]
    wide = left_hbm.shape[1]
    width, part = wide // 2, here_i // PARTS
    pieces = [
        pltpu.make_async_copy(
            pair_hbm.at[pl.ds(p * part, part)], pair_ref.at[pl.ds(p * part, part)], arrived.at[p]
        )
        for p in range(PARTS)
    ]
    small = [
        pltpu.make_async_copy(left_hbm, weights.at[0], arrived.at[PARTS]),
        pltpu.make_async_copy(right_hbm, weights.at[1], arrived.at[PARTS + 1]),
        pltpu.make_async_copy(gain_hbm, gain_ref, arrived.at[PARTS + 2]),
    ]
    for copy in pieces[:1] + small + pieces[1:]:
        copy.start()
    for copy in small:
        copy.wait()
    for side in range(2):
        turned[side * wide : (side + 1) * wide] = (0.5 * weights[side].astype(F32)).T.astype(BF16)
    gain = gain_ref[...]
    for start in range(0, here_i, STRIP):
        strip = start // STRIP
        for i in range(0, STRIP, 2):
            row = start + i
            if row % part == 0:
                pieces[row // part].wait()
            rows = pair_ref[row : row + 2].reshape(2 * here_k, channels).astype(F32)
            normed = normalize(rows, gain)
            both = lax.dot_general(
                turned[...], normed, (((1,), (1,)), ((), ())), preferred_element_type=F32
            )
            for side in range(2):
                one = both[side * wide : (side + 1) * wide]
                gated = (jnp.tanh(one[:width]) + 1.0) * one[width:]
                sides[strip, side, i] = gated[:, :here_k]
                sides[strip, side, i + 1] = gated[:, here_k:]
        for side in range(2):
            by_channel = jnp.swapaxes(sides[strip, side], 0, 1).astype(BF16)
            sent_ref[:, :, side, start : start + STRIP] = by_channel.reshape(
                chips, cols, STRIP, here_k
            )


def operands(pair, gain, proj_left, proj_right, chips, cols):
    here_i, here_k, channels = pair.shape
    wide = proj_left.shape[1]
    hbm = pl.BlockSpec(memory_space=pltpu.HBM)
    arrays = [
        pltpu.with_memory_space_constraint(array, pltpu.HBM)
        for array in (pair, gain, proj_left, proj_right)
    ]
    return pl.pallas_call(
        operands_kernel,
        in_specs=[hbm] * 4,
        out_specs=pl.BlockSpec(memory_space=pltpu.VMEM),
        out_shape=jax.ShapeDtypeStruct((chips, cols, 2, here_i, here_k), BF16),
        scratch_shapes=[
            pltpu.VMEM(pair.shape, BF16),
            pltpu.VMEM(gain.shape, F32),
            pltpu.VMEM((2, channels, wide), BF16),
            pltpu.VMEM((2 * wide, channels), BF16),
            pltpu.VMEM((here_i // STRIP, 2, STRIP, wide // 2, here_k), F32),
            pltpu.SemaphoreType.DMA((PARTS + 3,)),
        ],
        compiler_params=pltpu.CompilerParams(vmem_limit_bytes=VMEM_LIMIT),
        name="operands",
    )(*arrays)


def split_kernel(got_ref, right_ref):
    right_ref[...] = got_ref[:, :, 1]


def split(got):
    rows, cols, _, half, here_k = got.shape
    vmem = pl.BlockSpec(memory_space=pltpu.VMEM)
    return pl.pallas_call(
        split_kernel,
        in_specs=[vmem],
        out_specs=vmem,
        out_shape=jax.ShapeDtypeStruct((rows, cols, half, here_k), BF16),
        compiler_params=pltpu.CompilerParams(vmem_limit_bytes=VMEM_LIMIT),
        name="split",
    )(got)


def own_kernel(
    got_ref, pair_hbm, gain_hbm, weight_hbm, left_ref, own_ref, gate_ref,
    right, pair_ref, gain_ref, weight_ref, arrived,
):
    incoming = [
        pltpu.make_async_copy(source, target, arrived.at[n])
        for n, (source, target) in enumerate(
            ((weight_hbm, weight_ref), (gain_hbm, gain_ref), (pair_hbm, pair_ref))
        )
    ]
    for copy in incoming:
        copy.start()
    rows, cols, _, half, here_k = got_ref.shape
    for s in range(cols):
        span = pl.ds(s * here_k, here_k)
        left_ref[:, span] = got_ref[:, s, 0].reshape(rows * half, here_k)
        right[:, span] = got_ref[:, s, 1].reshape(rows * half, here_k)
    step = 2 * here_k
    for j in range(0, rows * half, step):
        own_ref[:, j : j + step] = lax.dot_general(
            left_ref[...], right[j : j + step], (((1,), (1,)), ((), ())), preferred_element_type=F32
        ).astype(BF16)
    for copy in incoming:
        copy.wait()
    weight = (0.5 * weight_ref[...].astype(F32)).astype(BF16)
    here_i, _, channels = pair_ref.shape
    for i in range(0, here_i, 4):
        some = pair_ref[i : i + 4].reshape(4 * here_k, channels).astype(F32)
        gate = jnp.dot(normalize(some, gain_ref[...]), weight, preferred_element_type=F32)
        gate_ref[i : i + 4] = (jnp.tanh(gate) + 1.0).reshape(4, here_k, channels)


def own_part(got, pair, gain, gate_weight):
    rows, cols, _, half, here_k = got.shape
    tall, deep = rows * half, cols * here_k
    vmem, hbm = pl.BlockSpec(memory_space=pltpu.VMEM), pl.BlockSpec(memory_space=pltpu.HBM)
    arrays = [
        pltpu.with_memory_space_constraint(array, pltpu.HBM) for array in (pair, gain, gate_weight)
    ]
    return pl.pallas_call(
        own_kernel,
        in_specs=[vmem, hbm, hbm, hbm],
        out_specs=[vmem, vmem, vmem],
        out_shape=[
            jax.ShapeDtypeStruct((tall, deep), BF16),
            jax.ShapeDtypeStruct((tall, tall), BF16),
            jax.ShapeDtypeStruct(pair.shape, F32),
        ],
        scratch_shapes=[
            pltpu.VMEM((tall, deep), BF16),
            pltpu.VMEM(pair.shape, BF16),
            pltpu.VMEM(gain.shape, F32),
            pltpu.VMEM(gate_weight.shape, BF16),
            pltpu.SemaphoreType.DMA((3,)),
        ],
        compiler_params=pltpu.CompilerParams(vmem_limit_bytes=VMEM_LIMIT),
        cost_estimate=pl.CostEstimate(
            flops=2 * tall * tall * deep, bytes_accessed=8 * tall * deep, transcendentals=pair.size
        ),
        name="own_part",
    )(got, *arrays)


def merge_kernel(left_ref, own_ref, other_ref, product_ref, right):
    rows, cols, half, here_k = other_ref.shape
    each = rows // cols * half
    for s in range(cols):
        span = pl.ds(s * here_k, here_k)
        block = other_ref[:, s].reshape(cols // 2, 2, each, here_k)
        right[:, 1, :, span] = block[:, 0]
        right[:, 0, :, span] = block[:, 1]
    first = lax.broadcasted_iota(jnp.int32, (1, here_k), 1) < each
    for pair in range(0, cols // 2, 2):
        part = right[pair : pair + 2].reshape(2 * here_k, cols * here_k)
        total = lax.dot_general(
            left_ref[...], part, (((1,), (1,)), ((), ())), preferred_element_type=F32
        )
        for p in range(2):
            span = pl.ds((pair + p) * here_k, here_k)
            own = own_ref[:, span].astype(F32)
            other = total[:, p * here_k : (p + 1) * here_k]
            even = jnp.where(first, own, other).astype(BF16)
            odd = jnp.where(first, other, own).astype(BF16)
            product_ref[:, 2 * (pair + p)] = even.reshape(rows, half, here_k)
            product_ref[:, 2 * (pair + p) + 1] = odd.reshape(rows, half, here_k)


def merge(left, own, other):
    rows, cols, half, here_k = other.shape
    vmem = pl.BlockSpec(memory_space=pltpu.VMEM)
    return pl.pallas_call(
        merge_kernel,
        in_specs=[vmem, vmem, vmem],
        out_specs=vmem,
        out_shape=jax.ShapeDtypeStruct(other.shape, BF16),
        scratch_shapes=[
            pltpu.VMEM((cols // 2, 2, rows // cols * half, cols * here_k), BF16),
        ],
        compiler_params=pltpu.CompilerParams(vmem_limit_bytes=VMEM_LIMIT),
        name="merge",
    )(left, own, other)


def update_kernel(
    first_ref, back_ref, gain_hbm, weight_hbm, gate_ref, update_hbm,
    gain_ref, weight_ref, update_ref, arrived, left,
):
    chips, cols, here_i, here_k = back_ref.shape
    width = chips * cols
    _, each, _, run, channels = gate_ref.shape
    first = first_ref[0]
    second = 1 - first
    incoming = [
        pltpu.make_async_copy(gain_hbm, gain_ref, arrived.at[0]),
        pltpu.make_async_copy(weight_hbm, weight_ref, arrived.at[1]),
    ]
    for copy in incoming:
        copy.start()
    outgoing = []
    for start in range(0, here_i, STRIP):
        product = back_ref[:, :, start : start + STRIP].reshape(width, STRIP, here_k).astype(F32)
        average = jnp.mean(product, axis=0, keepdims=True)
        centered = product - average
        spread = jnp.mean(centered * centered, axis=0, keepdims=True)
        normed = centered * lax.rsqrt(spread + 1e-05)
        if start == 0:
            for copy in incoming:
                copy.wait()
            gain = jnp.broadcast_to(gain_ref[...], (here_k, width)).T
            weight = (0.5 * weight_ref[...].astype(F32)).astype(BF16)
        normed = (jnp.swapaxes(normed, 0, 1) * gain).astype(BF16)
        for i in range(STRIP):
            row = start + i
            projected = lax.dot_general(
                normed[i], weight, (((0,), (0,)), ((), ())), preferred_element_type=F32
            ).reshape(2, each, run, channels)
            update_ref[row, :, first] = (gate_ref[row, :, first] * projected[0]).astype(BF16)
            update_ref[row, :, second] = (gate_ref[row, :, second] * projected[1]).astype(BF16)
            if (i + 1) % 4 == 0:
                span = pl.ds(row - 3, 4)
                copy = pltpu.make_async_copy(
                    update_ref.at[span], update_hbm.at[span], left.at[len(outgoing)]
                )
                copy.start()
                outgoing.append(copy)
    for copy in outgoing:
        copy.wait()


def updates(first, back, gain, weight, gate):
    here_i, here_k, channels = gate.shape
    blocked = (here_i, here_k // (2 * here_i), 2, here_i, channels)
    vmem, hbm = pl.BlockSpec(memory_space=pltpu.VMEM), pl.BlockSpec(memory_space=pltpu.HBM)
    gain, weight = (pltpu.with_memory_space_constraint(array, pltpu.HBM) for array in (gain, weight))
    update = pl.pallas_call(
        update_kernel,
        in_specs=[pl.BlockSpec(memory_space=pltpu.SMEM), vmem, hbm, hbm, vmem],
        out_specs=hbm,
        out_shape=jax.ShapeDtypeStruct(blocked, BF16),
        scratch_shapes=[
            pltpu.VMEM(gain.shape, F32),
            pltpu.VMEM(weight.shape, BF16),
            pltpu.VMEM(blocked, BF16),
            pltpu.SemaphoreType.DMA((2,)),
            pltpu.SemaphoreType.DMA((here_i // 4,)),
        ],
        compiler_params=pltpu.CompilerParams(vmem_limit_bytes=VMEM_LIMIT),
        name="updates",
    )(first, back, gain, weight, gate.reshape(blocked))
    return update.reshape(gate.shape)


def shards(chips, cols, pair, ln_in_gain, proj_left, proj_right, gate_weight, ln_out_gain, out_weight):
    width = out_weight.shape[0]
    here_i, here_k = pair.shape[0], pair.shape[1]
    exchange = functools.partial(
        lax.all_to_all, axis_name=("chip", "col"), split_axis=0, concat_axis=0, tiled=True
    )
    gain = ln_in_gain.reshape(1, -1)
    sent = operands(pair, gain, proj_left, proj_right, chips, cols)
    got = exchange(sent.reshape(chips * cols, 2, here_i, here_k))
    got = got.reshape(chips, cols, 2, here_i, here_k)
    other = lax.ppermute(split(got), "core", [(0, 1), (1, 0)])
    left, own, gate = own_part(got, pair, gain, gate_weight)
    product = merge(left, own, other)
    first = lax.rem(lax.axis_index("core") + lax.axis_index("col"), 2).reshape(1)
    product, first = lax.optimization_barrier((product, first))
    back = exchange(product.reshape(chips * cols, here_i, here_k))
    return updates(
        first, back.reshape(chips, cols, here_i, here_k), ln_out_gain.reshape(1, width), out_weight, gate
    )


def solution(mesh):
    rows, cols = mesh.shape["row"], mesh.shape["col"]
    chips = rows // 2
    by_core = jax.sharding.Mesh(mesh.devices.reshape(chips, 2, cols), ("chip", "core", "col"))
    cells = P(("chip", "core"), "col", None)
    step = functools.partial(shards, chips, cols)
    return jax.shard_map(
        step, mesh=by_core, in_specs=(cells,) + (P(),) * 6, out_specs=cells, check_vma=False
    )
```

```python
import functools

import jax
import jax.numpy as jnp
from jax import lax
from jax.experimental import pallas as pl
from jax.experimental.pallas import tpu as pltpu
from jax.sharding import PartitionSpec as P

F32, BF16 = jnp.float32, jnp.bfloat16
VMEM_LIMIT = 40 * 1024 * 1024


def sigmoid(values):
    return 0.5 * jnp.tanh(0.5 * values) + 0.5


def normalize(values, gain):
    average = jnp.mean(values, axis=-1, keepdims=True)
    centered = values - average
    spread = jnp.mean(centered * centered, axis=-1, keepdims=True)
    return (centered * lax.rsqrt(spread + 1e-05) * gain).astype(BF16)


PARTS = 4
STRIP = 16


def operands_kernel(
    pair_hbm, gain_hbm, left_hbm, right_hbm, sent_hbm,
    sent_ref, pair_ref, gain_ref, weights, turned, sides, arrived, left,
):
    here_i, here_k, channels = pair_ref.shape
    chips, cols = sent_ref.shape[:2]
    wide = left_hbm.shape[1]
    width, part = wide // 2, here_i // PARTS
    pieces = [
        pltpu.make_async_copy(
            pair_hbm.at[pl.ds(p * part, part)], pair_ref.at[pl.ds(p * part, part)], arrived.at[p]
        )
        for p in range(PARTS)
    ]
    small = [
        pltpu.make_async_copy(left_hbm, weights.at[0], arrived.at[PARTS]),
        pltpu.make_async_copy(right_hbm, weights.at[1], arrived.at[PARTS + 1]),
        pltpu.make_async_copy(gain_hbm, gain_ref, arrived.at[PARTS + 2]),
    ]
    for copy in pieces[:1] + small + pieces[1:]:
        copy.start()
    for copy in small:
        copy.wait()
    for side in range(2):
        turned[side * wide : (side + 1) * wide] = (0.5 * weights[side].astype(F32)).T.astype(BF16)
    gain = gain_ref[...]
    outgoing = []
    for start in range(0, here_i, STRIP):
        strip = start // STRIP
        for i in range(0, STRIP, 2):
            row = start + i
            if row % part == 0:
                pieces[row // part].wait()
            rows = pair_ref[row : row + 2].reshape(2 * here_k, channels).astype(F32)
            normed = normalize(rows, gain)
            both = lax.dot_general(
                turned[...], normed, (((1,), (1,)), ((), ())), preferred_element_type=F32
            )
            for side in range(2):
                one = both[side * wide : (side + 1) * wide]
                gated = (jnp.tanh(one[:width]) + 1.0) * one[width:]
                sides[strip, side, i] = gated[:, :here_k]
                sides[strip, side, i + 1] = gated[:, here_k:]
        for side in range(2):
            by_channel = jnp.swapaxes(sides[strip, side], 0, 1).astype(BF16)
            sent_ref[:, :, side, start : start + STRIP] = by_channel.reshape(
                chips, cols, STRIP, here_k
            )
            span = pl.ds(start, STRIP)
            copy = pltpu.make_async_copy(
                sent_ref.at[:, :, side, span], sent_hbm.at[:, :, side, span], left.at[len(outgoing)]
            )
            copy.start()
            outgoing.append(copy)
    for copy in outgoing:
        copy.wait()


def operands(pair, gain, proj_left, proj_right, chips, cols):
    here_i, here_k, channels = pair.shape
    wide = proj_left.shape[1]
    hbm = pl.BlockSpec(memory_space=pltpu.HBM)
    arrays = [
        pltpu.with_memory_space_constraint(array, pltpu.HBM)
        for array in (pair, gain, proj_left, proj_right)
    ]
    return pl.pallas_call(
        operands_kernel,
        in_specs=[hbm] * 4,
        out_specs=hbm,
        out_shape=pltpu.HBM((chips, cols, 2, here_i, here_k), BF16),
        scratch_shapes=[
            pltpu.VMEM((chips, cols, 2, here_i, here_k), BF16),
            pltpu.VMEM(pair.shape, BF16),
            pltpu.VMEM(gain.shape, F32),
            pltpu.VMEM((2, channels, wide), BF16),
            pltpu.VMEM((2 * wide, channels), BF16),
            pltpu.VMEM((here_i // STRIP, 2, STRIP, wide // 2, here_k), F32),
            pltpu.SemaphoreType.DMA((PARTS + 3,)),
            pltpu.SemaphoreType.DMA((2 * here_i // STRIP,)),
        ],
        compiler_params=pltpu.CompilerParams(vmem_limit_bytes=VMEM_LIMIT),
        name="operands",
    )(*arrays)


def split_kernel(got_ref, right_ref):
    right_ref[...] = got_ref[:, :, 1]


def split(got):
    rows, cols, _, half, here_k = got.shape
    vmem = pl.BlockSpec(memory_space=pltpu.VMEM)
    return pl.pallas_call(
        split_kernel,
        in_specs=[vmem],
        out_specs=vmem,
        out_shape=jax.ShapeDtypeStruct((rows, cols, half, here_k), BF16),
        compiler_params=pltpu.CompilerParams(vmem_limit_bytes=VMEM_LIMIT),
        name="split",
    )(got)


def own_kernel(got_ref, left_ref, own_ref, right):
    rows, cols, _, half, here_k = got_ref.shape
    for s in range(cols):
        span = pl.ds(s * here_k, here_k)
        left_ref[:, span] = got_ref[:, s, 0].reshape(rows * half, here_k)
        right[:, span] = got_ref[:, s, 1].reshape(rows * half, here_k)
    step = 2 * here_k
    for j in range(0, rows * half, step):
        own_ref[:, j : j + step] = lax.dot_general(
            left_ref[...], right[j : j + step], (((1,), (1,)), ((), ())), preferred_element_type=F32
        ).astype(BF16)


def own_part(got):
    rows, cols, _, half, here_k = got.shape
    tall, deep = rows * half, cols * here_k
    vmem = pl.BlockSpec(memory_space=pltpu.VMEM)
    return pl.pallas_call(
        own_kernel,
        in_specs=[vmem],
        out_specs=[vmem, vmem],
        out_shape=[
            jax.ShapeDtypeStruct((tall, deep), BF16),
            jax.ShapeDtypeStruct((tall, tall), BF16),
        ],
        scratch_shapes=[pltpu.VMEM((tall, deep), BF16)],
        compiler_params=pltpu.CompilerParams(vmem_limit_bytes=VMEM_LIMIT),
        cost_estimate=pl.CostEstimate(
            flops=2 * tall * tall * deep, bytes_accessed=8 * tall * deep, transcendentals=0
        ),
        name="own_part",
    )(got)


def merge_kernel(left_ref, own_ref, other_ref, product_hbm, product_ref, right, left):
    rows, cols, half, here_k = other_ref.shape
    each = rows // cols * half
    for s in range(cols):
        span = pl.ds(s * here_k, here_k)
        block = other_ref[:, s].reshape(cols // 2, 2, each, here_k)
        right[:, 1, :, span] = block[:, 0]
        right[:, 0, :, span] = block[:, 1]
    outgoing = []
    first = lax.broadcasted_iota(jnp.int32, (1, here_k), 1) < each
    for pair in range(0, cols // 2, 2):
        part = right[pair : pair + 2].reshape(2 * here_k, cols * here_k)
        total = lax.dot_general(
            left_ref[...], part, (((1,), (1,)), ((), ())), preferred_element_type=F32
        )
        for p in range(2):
            span = pl.ds((pair + p) * here_k, here_k)
            own = own_ref[:, span].astype(F32)
            other = total[:, p * here_k : (p + 1) * here_k]
            even = jnp.where(first, own, other).astype(BF16)
            odd = jnp.where(first, other, own).astype(BF16)
            product_ref[:, 2 * (pair + p)] = even.reshape(rows, half, here_k)
            product_ref[:, 2 * (pair + p) + 1] = odd.reshape(rows, half, here_k)
            span = pl.ds(2 * (pair + p), 2)
            copy = pltpu.make_async_copy(
                product_ref.at[:, span], product_hbm.at[:, span], left.at[pair + p]
            )
            copy.start()
            outgoing.append(copy)
    for copy in outgoing:
        copy.wait()


def merge(left, own, other):
    rows, cols, half, here_k = other.shape
    vmem = pl.BlockSpec(memory_space=pltpu.VMEM)
    return pl.pallas_call(
        merge_kernel,
        in_specs=[vmem, vmem, vmem],
        out_specs=pl.BlockSpec(memory_space=pltpu.HBM),
        out_shape=pltpu.HBM(other.shape, BF16),
        scratch_shapes=[
            pltpu.VMEM(other.shape, BF16),
            pltpu.VMEM((cols // 2, 2, rows // cols * half, cols * here_k), BF16),
            pltpu.SemaphoreType.DMA((cols // 2,)),
        ],
        compiler_params=pltpu.CompilerParams(vmem_limit_bytes=VMEM_LIMIT),
        name="merge",
    )(left, own, other)


def gate_kernel(pair_ref, gain_ref, weight_ref, gate_ref):
    some, here_k, channels = pair_ref.shape
    rows = pair_ref[...].reshape(some * here_k, channels).astype(F32)
    normed = normalize(rows, gain_ref[...])
    gate = sigmoid(jnp.dot(normed, weight_ref[...], preferred_element_type=F32))
    gate_ref[...] = gate.reshape(gate_ref.shape)


def gates(pair, gain, weight):
    here_i, here_k, channels = pair.shape
    some = here_i // 4
    block = pl.BlockSpec((some, here_k, channels), lambda i: (i, 0, 0))
    return pl.pallas_call(
        gate_kernel,
        grid=(4,),
        in_specs=[
            block,
            pl.BlockSpec(gain.shape, lambda i: (0, 0)),
            pl.BlockSpec(weight.shape, lambda i: (0, 0)),
        ],
        out_specs=block,
        out_shape=jax.ShapeDtypeStruct(pair.shape, F32),
        compiler_params=pltpu.CompilerParams(vmem_limit_bytes=VMEM_LIMIT),
        cost_estimate=pl.CostEstimate(
            flops=2 * pair.size * channels, bytes_accessed=6 * pair.size, transcendentals=pair.size
        ),
        name="gates",
    )(pair, gain, weight)


def update_kernel(
    first_ref, back_ref, gain_ref, weight_ref, gate_ref, update_hbm, update_ref, left
):
    chips, cols, here_i, here_k = back_ref.shape
    width = chips * cols
    _, each, _, run, channels = gate_ref.shape
    first = first_ref[0]
    second = 1 - first
    gain = jnp.broadcast_to(gain_ref[...], (here_k, width)).T
    outgoing = []
    for start in range(0, here_i, STRIP):
        product = back_ref[:, :, start : start + STRIP].reshape(width, STRIP, here_k).astype(F32)
        average = jnp.mean(product, axis=0, keepdims=True)
        centered = product - average
        spread = jnp.mean(centered * centered, axis=0, keepdims=True)
        normed = centered * lax.rsqrt(spread + 1e-05)
        normed = (jnp.swapaxes(normed, 0, 1) * gain).astype(BF16)
        for i in range(STRIP):
            row = start + i
            projected = lax.dot_general(
                normed[i], weight_ref[...], (((0,), (0,)), ((), ())), preferred_element_type=F32
            ).reshape(2, each, run, channels)
            update_ref[row, :, first] = (gate_ref[row, :, first] * projected[0]).astype(BF16)
            update_ref[row, :, second] = (gate_ref[row, :, second] * projected[1]).astype(BF16)
            if (i + 1) % 4 == 0:
                span = pl.ds(row - 3, 4)
                copy = pltpu.make_async_copy(
                    update_ref.at[span], update_hbm.at[span], left.at[len(outgoing)]
                )
                copy.start()
                outgoing.append(copy)
    for copy in outgoing:
        copy.wait()


def updates(first, back, gain, weight, gate):
    here_i, here_k, channels = gate.shape
    blocked = (here_i, here_k // (2 * here_i), 2, here_i, channels)
    vmem, hbm = pl.BlockSpec(memory_space=pltpu.VMEM), pl.BlockSpec(memory_space=pltpu.HBM)
    update = pl.pallas_call(
        update_kernel,
        in_specs=[pl.BlockSpec(memory_space=pltpu.SMEM), vmem, vmem, vmem, vmem],
        out_specs=hbm,
        out_shape=jax.ShapeDtypeStruct(blocked, BF16),
        scratch_shapes=[
            pltpu.VMEM(blocked, BF16),
            pltpu.SemaphoreType.DMA((here_i // 4,)),
        ],
        compiler_params=pltpu.CompilerParams(vmem_limit_bytes=VMEM_LIMIT),
        name="updates",
    )(first, back, gain, weight, gate.reshape(blocked))
    return update.reshape(gate.shape)


def shards(chips, cols, pair, ln_in_gain, proj_left, proj_right, gate_weight, ln_out_gain, out_weight):
    width = out_weight.shape[0]
    here_i, here_k = pair.shape[0], pair.shape[1]
    exchange = functools.partial(
        lax.all_to_all, axis_name=("chip", "col"), split_axis=0, concat_axis=0, tiled=True
    )
    gain = ln_in_gain.reshape(1, -1)
    sent = operands(pair, gain, proj_left, proj_right, chips, cols)
    sent, late_pair = lax.optimization_barrier((sent, pair))
    got = exchange(sent.reshape(chips * cols, 2, here_i, here_k))
    gate = gates(late_pair, gain, gate_weight)
    got, gate = lax.optimization_barrier((got, gate))
    got = got.reshape(chips, cols, 2, here_i, here_k)
    other = lax.ppermute(split(got), "core", [(0, 1), (1, 0)])
    left, own = own_part(got)
    product = merge(left, own, other)
    back = exchange(product.reshape(chips * cols, here_i, here_k))
    first = lax.rem(lax.axis_index("core") + lax.axis_index("col"), 2).reshape(1)
    return updates(
        first, back.reshape(chips, cols, here_i, here_k), ln_out_gain.reshape(1, width), out_weight, gate
    )


def solution(mesh):
    rows, cols = mesh.shape["row"], mesh.shape["col"]
    chips = rows // 2
    by_core = jax.sharding.Mesh(mesh.devices.reshape(chips, 2, cols), ("chip", "core", "col"))
    cells = P(("chip", "core"), "col", None)
    step = functools.partial(shards, chips, cols)
    return jax.shard_map(
        step, mesh=by_core, in_specs=(cells,) + (P(),) * 6, out_specs=cells, check_vma=False
    )
```

```python
import functools

import jax
import jax.numpy as jnp
from jax import lax
from jax.experimental import pallas as pl
from jax.experimental.pallas import tpu as pltpu
from jax.sharding import PartitionSpec as P

F32, BF16 = jnp.float32, jnp.bfloat16
VMEM_LIMIT = 40 * 1024 * 1024


def sigmoid(values):
    return 0.5 * jnp.tanh(0.5 * values) + 0.5


def normalize(values, gain, axis):
    average = jnp.mean(values, axis=axis, keepdims=True)
    centered = values - average
    spread = jnp.mean(centered * centered, axis=axis, keepdims=True)
    return (centered * lax.rsqrt(spread + 1e-05) * gain).astype(BF16)


PARTS = 4


def operands_kernel(
    pair_hbm, gain_hbm, left_hbm, right_hbm, sent_ref, pair_ref, gain_ref, weights, turned, sides, arrived
):
    here_i, here_k, channels = pair_ref.shape
    chips, cores, cols, _, half, _ = sent_ref.shape
    wide = left_hbm.shape[1]
    width, part = wide // 2, here_i // PARTS
    pieces = [
        pltpu.make_async_copy(
            pair_hbm.at[pl.ds(p * part, part)], pair_ref.at[pl.ds(p * part, part)], arrived.at[p]
        )
        for p in range(PARTS)
    ]
    small = [
        pltpu.make_async_copy(left_hbm, weights.at[0], arrived.at[PARTS]),
        pltpu.make_async_copy(right_hbm, weights.at[1], arrived.at[PARTS + 1]),
        pltpu.make_async_copy(gain_hbm, gain_ref, arrived.at[PARTS + 2]),
    ]
    for copy in pieces[:1] + small + pieces[1:]:
        copy.start()
    for copy in small:
        copy.wait()
    for side in range(2):
        turned[side * wide : (side + 1) * wide] = (0.5 * weights[side].astype(F32)).T.astype(BF16)
    gain = jnp.broadcast_to(gain_ref[...], (2 * here_k, channels)).T
    for core in range(cores):
        for i in range(0, half, 2):
            row = core * half + i
            if row % part == 0:
                pieces[row // part].wait()
            turned_rows = pair_ref[row : row + 2].reshape(2 * here_k, channels).T.astype(F32)
            normed = normalize(turned_rows, gain, 0)
            both = lax.dot_general(
                turned[...], normed, (((1,), (0,)), ((), ())), preferred_element_type=F32
            )
            for side in range(2):
                one = both[side * wide : (side + 1) * wide]
                gated = (jnp.tanh(one[:width]) + 1.0) * one[width:]
                sides[core, side, i] = gated[:, :here_k]
                sides[core, side, i + 1] = gated[:, here_k:]
        for side in range(2):
            by_channel = jnp.swapaxes(sides[core, side], 0, 1).astype(BF16)
            sent_ref[:, core, :, side] = by_channel.reshape(chips, cols, half, here_k)


def operands(pair, gain, proj_left, proj_right, chips, cols):
    here_i, here_k, channels = pair.shape
    half, wide = here_i // 2, proj_left.shape[1]
    hbm = pl.BlockSpec(memory_space=pltpu.HBM)
    arrays = [
        pltpu.with_memory_space_constraint(array, pltpu.HBM)
        for array in (pair, gain, proj_left, proj_right)
    ]
    return pl.pallas_call(
        operands_kernel,
        in_specs=[hbm] * 4,
        out_specs=pl.BlockSpec(memory_space=pltpu.VMEM),
        out_shape=jax.ShapeDtypeStruct((chips, 2, cols, 2, half, here_k), BF16),
        scratch_shapes=[
            pltpu.VMEM(pair.shape, BF16),
            pltpu.VMEM(gain.shape, F32),
            pltpu.VMEM((2, channels, wide), BF16),
            pltpu.VMEM((2 * wide, channels), BF16),
            pltpu.VMEM((2, 2, half, wide // 2, here_k), F32),
            pltpu.SemaphoreType.DMA((PARTS + 3,)),
        ],
        compiler_params=pltpu.CompilerParams(vmem_limit_bytes=VMEM_LIMIT),
        name="operands",
    )(*arrays)


def split_kernel(got_ref, right_ref):
    right_ref[...] = got_ref[:, :, 1]


def split(got):
    rows, cols, _, half, here_k = got.shape
    vmem = pl.BlockSpec(memory_space=pltpu.VMEM)
    return pl.pallas_call(
        split_kernel,
        in_specs=[vmem],
        out_specs=vmem,
        out_shape=jax.ShapeDtypeStruct((rows, cols, half, here_k), BF16),
        compiler_params=pltpu.CompilerParams(vmem_limit_bytes=VMEM_LIMIT),
        name="split",
    )(got)


def own_kernel(got_ref, left_ref, own_ref, right):
    rows, cols, _, half, here_k = got_ref.shape
    for s in range(cols):
        span = pl.ds(s * here_k, here_k)
        left_ref[:, span] = got_ref[:, s, 0].reshape(rows * half, here_k)
        right[:, span] = got_ref[:, s, 1].reshape(rows * half, here_k)
    step = 2 * here_k
    for j in range(0, rows * half, step):
        own_ref[:, j : j + step] = lax.dot_general(
            left_ref[...], right[j : j + step], (((1,), (1,)), ((), ())), preferred_element_type=F32
        ).astype(BF16)


def own_part(got):
    rows, cols, _, half, here_k = got.shape
    tall, deep = rows * half, cols * here_k
    vmem = pl.BlockSpec(memory_space=pltpu.VMEM)
    return pl.pallas_call(
        own_kernel,
        in_specs=[vmem],
        out_specs=[vmem, vmem],
        out_shape=[
            jax.ShapeDtypeStruct((tall, deep), BF16),
            jax.ShapeDtypeStruct((tall, tall), BF16),
        ],
        scratch_shapes=[pltpu.VMEM((tall, deep), BF16)],
        compiler_params=pltpu.CompilerParams(vmem_limit_bytes=VMEM_LIMIT),
        cost_estimate=pl.CostEstimate(
            flops=2 * tall * tall * deep, bytes_accessed=8 * tall * deep, transcendentals=0
        ),
        name="own_part",
    )(got)


def merge_kernel(left_ref, own_ref, other_ref, product_hbm, product_ref, right, left):
    rows, cols, half, here_k = other_ref.shape
    each = rows // cols * half
    for s in range(cols):
        span = pl.ds(s * here_k, here_k)
        block = other_ref[:, s].reshape(cols // 2, 2, each, here_k)
        right[:, 1, :, span] = block[:, 0]
        right[:, 0, :, span] = block[:, 1]
    outgoing = []
    first = lax.broadcasted_iota(jnp.int32, (1, here_k), 1) < each
    for pair in range(0, cols // 2, 2):
        part = right[pair : pair + 2].reshape(2 * here_k, cols * here_k)
        total = lax.dot_general(
            left_ref[...], part, (((1,), (1,)), ((), ())), preferred_element_type=F32
        )
        for p in range(2):
            span = pl.ds((pair + p) * here_k, here_k)
            own = own_ref[:, span].astype(F32)
            other = total[:, p * here_k : (p + 1) * here_k]
            even = jnp.where(first, own, other).astype(BF16)
            odd = jnp.where(first, other, own).astype(BF16)
            product_ref[:, 2 * (pair + p)] = even.reshape(rows, half, here_k)
            product_ref[:, 2 * (pair + p) + 1] = odd.reshape(rows, half, here_k)
            span = pl.ds(2 * (pair + p), 2)
            copy = pltpu.make_async_copy(
                product_ref.at[:, span], product_hbm.at[:, span], left.at[pair + p]
            )
            copy.start()
            outgoing.append(copy)
    for copy in outgoing:
        copy.wait()


def merge(left, own, other):
    rows, cols, half, here_k = other.shape
    vmem = pl.BlockSpec(memory_space=pltpu.VMEM)
    return pl.pallas_call(
        merge_kernel,
        in_specs=[vmem, vmem, vmem],
        out_specs=pl.BlockSpec(memory_space=pltpu.HBM),
        out_shape=jax.ShapeDtypeStruct(other.shape, BF16),
        scratch_shapes=[
            pltpu.VMEM(other.shape, BF16),
            pltpu.VMEM((cols // 2, 2, rows // cols * half, cols * here_k), BF16),
            pltpu.SemaphoreType.DMA((cols // 2,)),
        ],
        compiler_params=pltpu.CompilerParams(vmem_limit_bytes=VMEM_LIMIT),
        name="merge",
    )(left, own, other)


def gate_kernel(pair_ref, gain_ref, weight_ref, gate_ref):
    some, here_k, channels = pair_ref.shape
    rows = pair_ref[...].reshape(some * here_k, channels).astype(F32)
    normed = normalize(rows, gain_ref[...], 1)
    gate = sigmoid(jnp.dot(normed, weight_ref[...], preferred_element_type=F32))
    gate_ref[...] = gate.reshape(gate_ref.shape)


def gates(pair, gain, weight):
    here_i, here_k, channels = pair.shape
    some = here_i // 4
    block = pl.BlockSpec((some, here_k, channels), lambda i: (i, 0, 0))
    return pl.pallas_call(
        gate_kernel,
        grid=(4,),
        in_specs=[
            block,
            pl.BlockSpec(gain.shape, lambda i: (0, 0)),
            pl.BlockSpec(weight.shape, lambda i: (0, 0)),
        ],
        out_specs=block,
        out_shape=jax.ShapeDtypeStruct(pair.shape, F32),
        compiler_params=pltpu.CompilerParams(vmem_limit_bytes=VMEM_LIMIT),
        cost_estimate=pl.CostEstimate(
            flops=2 * pair.size * channels, bytes_accessed=6 * pair.size, transcendentals=pair.size
        ),
        name="gates",
    )(pair, gain, weight)


def update_kernel(
    odd_ref, back_ref, gain_ref, weight_ref, gate_ref, update_hbm, update_ref, left
):
    chips, cores, cols, half, here_k = back_ref.shape
    width, each = chips * cols, gate_ref.shape[1]
    channels = gate_ref.shape[4]
    odd = odd_ref[0]
    gain = jnp.broadcast_to(gain_ref[...], (here_k, width)).T
    outgoing = []
    for c in range(cores):
        product = back_ref[:, c].reshape(width, half, here_k).astype(F32)
        average = jnp.mean(product, axis=0, keepdims=True)
        centered = product - average
        spread = jnp.mean(centered * centered, axis=0, keepdims=True)
        normed = centered * lax.rsqrt(spread + 1e-05)
        normed = (jnp.swapaxes(normed, 0, 1) * gain).astype(BF16)
        first = (c + odd) % 2
        for i in range(half):
            row = c * half + i
            projected = lax.dot_general(
                normed[i], weight_ref[...], (((0,), (0,)), ((), ())), preferred_element_type=F32
            ).reshape(2, each, half, channels)
            update_ref[row, :, first] = (gate_ref[row, :, first] * projected[0]).astype(BF16)
            second = 1 - first
            update_ref[row, :, second] = (gate_ref[row, :, second] * projected[1]).astype(BF16)
            if (i + 1) % 4 == 0:
                span = pl.ds(row - 3, 4)
                copy = pltpu.make_async_copy(
                    update_ref.at[span], update_hbm.at[span], left.at[len(outgoing)]
                )
                copy.start()
                outgoing.append(copy)
    for copy in outgoing:
        copy.wait()


def updates(odd, back, gain, weight, gate):
    chips, _, cols, half, here_k = back.shape
    here_i, _, channels = gate.shape
    blocked = (here_i, here_k // (2 * half), 2, half, channels)
    vmem, hbm = pl.BlockSpec(memory_space=pltpu.VMEM), pl.BlockSpec(memory_space=pltpu.HBM)
    update = pl.pallas_call(
        update_kernel,
        in_specs=[pl.BlockSpec(memory_space=pltpu.SMEM), vmem, vmem, vmem, vmem],
        out_specs=hbm,
        out_shape=jax.ShapeDtypeStruct(blocked, BF16),
        scratch_shapes=[
            pltpu.VMEM(blocked, BF16),
            pltpu.SemaphoreType.DMA((here_i // 4,)),
        ],
        compiler_params=pltpu.CompilerParams(vmem_limit_bytes=VMEM_LIMIT),
        name="updates",
    )(odd, back, gain, weight, gate.reshape(blocked))
    return update.reshape(gate.shape)


def shards(rows, cols, pair, ln_in_gain, proj_left, proj_right, gate_weight, ln_out_gain, out_weight):
    width = out_weight.shape[0]
    here_i, here_k = pair.shape[0], pair.shape[1]
    half, chips = here_i // 2, rows // 2
    both = ("row", "col")
    exchange = functools.partial(
        lax.all_to_all, axis_name=both, split_axis=0, concat_axis=0, tiled=True
    )
    gain = ln_in_gain.reshape(1, -1)
    sent = operands(pair, gain, proj_left, proj_right, chips, cols)
    got = exchange(sent.reshape(rows * cols, 2, half, here_k))
    got = got.reshape(rows, cols, 2, half, here_k)
    other = lax.ppermute(split(got), "row", [(r, r ^ 1) for r in range(rows)])
    left, own = own_part(got)
    product = merge(left, own, other)
    product, late_pair = lax.optimization_barrier((product, pair))
    back = exchange(product.reshape(rows * cols, half, here_k))
    gate = gates(late_pair, gain, gate_weight)
    odd = lax.rem(lax.axis_index("col"), 2).reshape(1)
    return updates(
        odd, back.reshape(chips, 2, cols, half, here_k), ln_out_gain.reshape(1, width), out_weight, gate
    )


def solution(mesh):
    rows, cols = mesh.shape["row"], mesh.shape["col"]
    in_specs = (P("row", "col", None), P(), P(), P(), P(), P(), P())
    out_specs = P("row", "col", None)
    step = functools.partial(shards, rows, cols)
    return jax.shard_map(step, mesh=mesh, in_specs=in_specs, out_specs=out_specs, check_vma=False)
```

```python
import functools

import jax
import jax.numpy as jnp
from jax import lax
from jax.experimental import pallas as pl
from jax.experimental.pallas import tpu as pltpu
from jax.sharding import PartitionSpec as P

F32, BF16 = jnp.float32, jnp.bfloat16
VMEM_LIMIT = 40 * 1024 * 1024


def sigmoid(values):
    return 0.5 * jnp.tanh(0.5 * values) + 0.5


def normalize(values, gain, axis):
    average = jnp.mean(values, axis=axis, keepdims=True)
    centered = values - average
    spread = jnp.mean(centered * centered, axis=axis, keepdims=True)
    return (centered * lax.rsqrt(spread + 1e-05) * gain).astype(BF16)


PARTS = 2


def operands_kernel(
    pair_hbm, gain_hbm, left_hbm, right_hbm, sent_ref, pair_ref, gain_ref, weights, turned, sides, arrived
):
    here_i, here_k, channels = pair_ref.shape
    chips, cores, cols, _, half, _ = sent_ref.shape
    wide = left_hbm.shape[1]
    width, part = wide // 2, here_i // PARTS
    pieces = [
        pltpu.make_async_copy(
            pair_hbm.at[pl.ds(p * part, part)], pair_ref.at[pl.ds(p * part, part)], arrived.at[p]
        )
        for p in range(PARTS)
    ]
    small = [
        pltpu.make_async_copy(left_hbm, weights.at[0], arrived.at[PARTS]),
        pltpu.make_async_copy(right_hbm, weights.at[1], arrived.at[PARTS + 1]),
        pltpu.make_async_copy(gain_hbm, gain_ref, arrived.at[PARTS + 2]),
    ]
    for copy in pieces[:1] + small + pieces[1:]:
        copy.start()
    for copy in small:
        copy.wait()
    for side in range(2):
        turned[side * wide : (side + 1) * wide] = (0.5 * weights[side].astype(F32)).T.astype(BF16)
    gain = jnp.broadcast_to(gain_ref[...], (2 * here_k, channels)).T
    for core in range(cores):
        for i in range(0, half, 2):
            row = core * half + i
            if row % part == 0:
                pieces[row // part].wait()
            turned_rows = pair_ref[row : row + 2].reshape(2 * here_k, channels).T.astype(F32)
            normed = normalize(turned_rows, gain, 0)
            both = lax.dot_general(
                turned[...], normed, (((1,), (0,)), ((), ())), preferred_element_type=F32
            )
            for side in range(2):
                one = both[side * wide : (side + 1) * wide]
                gated = (jnp.tanh(one[:width]) + 1.0) * one[width:]
                sides[core, side, i] = gated[:, :here_k]
                sides[core, side, i + 1] = gated[:, here_k:]
        for side in range(2):
            by_channel = jnp.swapaxes(sides[core, side], 0, 1).astype(BF16)
            sent_ref[:, core, :, side] = by_channel.reshape(chips, cols, half, here_k)


def operands(pair, gain, proj_left, proj_right, chips, cols):
    here_i, here_k, channels = pair.shape
    half, wide = here_i // 2, proj_left.shape[1]
    hbm = pl.BlockSpec(memory_space=pltpu.HBM)
    arrays = [
        pltpu.with_memory_space_constraint(array, pltpu.HBM)
        for array in (pair, gain, proj_left, proj_right)
    ]
    return pl.pallas_call(
        operands_kernel,
        in_specs=[hbm] * 4,
        out_specs=pl.BlockSpec(memory_space=pltpu.VMEM),
        out_shape=jax.ShapeDtypeStruct((chips, 2, cols, 2, half, here_k), BF16),
        scratch_shapes=[
            pltpu.VMEM(pair.shape, BF16),
            pltpu.VMEM(gain.shape, F32),
            pltpu.VMEM((2, channels, wide), BF16),
            pltpu.VMEM((2 * wide, channels), BF16),
            pltpu.VMEM((2, 2, half, wide // 2, here_k), F32),
            pltpu.SemaphoreType.DMA((PARTS + 3,)),
        ],
        compiler_params=pltpu.CompilerParams(vmem_limit_bytes=VMEM_LIMIT),
        name="operands",
    )(*arrays)


def split_kernel(got_ref, right_ref):
    right_ref[...] = got_ref[:, :, 1]


def split(got):
    rows, cols, _, half, here_k = got.shape
    vmem = pl.BlockSpec(memory_space=pltpu.VMEM)
    return pl.pallas_call(
        split_kernel,
        in_specs=[vmem],
        out_specs=vmem,
        out_shape=jax.ShapeDtypeStruct((rows, cols, half, here_k), BF16),
        compiler_params=pltpu.CompilerParams(vmem_limit_bytes=VMEM_LIMIT),
        name="split",
    )(got)


def own_kernel(got_ref, left_ref, own_ref, right):
    rows, cols, _, half, here_k = got_ref.shape
    for s in range(cols):
        span = pl.ds(s * here_k, here_k)
        left_ref[:, span] = got_ref[:, s, 0].reshape(rows * half, here_k)
        right[:, span] = got_ref[:, s, 1].reshape(rows * half, here_k)
    step = 2 * here_k
    for j in range(0, rows * half, step):
        own_ref[:, j : j + step] = lax.dot_general(
            left_ref[...], right[j : j + step], (((1,), (1,)), ((), ())), preferred_element_type=F32
        ).astype(BF16)


def own_part(got):
    rows, cols, _, half, here_k = got.shape
    tall, deep = rows * half, cols * here_k
    vmem = pl.BlockSpec(memory_space=pltpu.VMEM)
    return pl.pallas_call(
        own_kernel,
        in_specs=[vmem],
        out_specs=[vmem, vmem],
        out_shape=[
            jax.ShapeDtypeStruct((tall, deep), BF16),
            jax.ShapeDtypeStruct((tall, tall), BF16),
        ],
        scratch_shapes=[pltpu.VMEM((tall, deep), BF16)],
        compiler_params=pltpu.CompilerParams(vmem_limit_bytes=VMEM_LIMIT),
        cost_estimate=pl.CostEstimate(
            flops=2 * tall * tall * deep, bytes_accessed=8 * tall * deep, transcendentals=0
        ),
        name="own_part",
    )(got)


def merge_kernel(left_ref, own_ref, other_ref, product_hbm, product_ref, right, left):
    rows, cols, half, here_k = other_ref.shape
    each = rows // cols * half
    for s in range(cols):
        span = pl.ds(s * here_k, here_k)
        block = other_ref[:, s].reshape(cols // 2, 2, each, here_k)
        right[:, 1, :, span] = block[:, 0]
        right[:, 0, :, span] = block[:, 1]
    outgoing = []
    first = lax.broadcasted_iota(jnp.int32, (1, here_k), 1) < each
    for pair in range(0, cols // 2, 2):
        part = right[pair : pair + 2].reshape(2 * here_k, cols * here_k)
        total = lax.dot_general(
            left_ref[...], part, (((1,), (1,)), ((), ())), preferred_element_type=F32
        )
        for p in range(2):
            span = pl.ds((pair + p) * here_k, here_k)
            own = own_ref[:, span].astype(F32)
            other = total[:, p * here_k : (p + 1) * here_k]
            even = jnp.where(first, own, other).astype(BF16)
            odd = jnp.where(first, other, own).astype(BF16)
            product_ref[:, 2 * (pair + p)] = even.reshape(rows, half, here_k)
            product_ref[:, 2 * (pair + p) + 1] = odd.reshape(rows, half, here_k)
            span = pl.ds(2 * (pair + p), 2)
            copy = pltpu.make_async_copy(
                product_ref.at[:, span], product_hbm.at[:, span], left.at[pair + p]
            )
            copy.start()
            outgoing.append(copy)
    for copy in outgoing:
        copy.wait()


def merge(left, own, other):
    rows, cols, half, here_k = other.shape
    vmem = pl.BlockSpec(memory_space=pltpu.VMEM)
    return pl.pallas_call(
        merge_kernel,
        in_specs=[vmem, vmem, vmem],
        out_specs=pl.BlockSpec(memory_space=pltpu.HBM),
        out_shape=jax.ShapeDtypeStruct(other.shape, BF16),
        scratch_shapes=[
            pltpu.VMEM(other.shape, BF16),
            pltpu.VMEM((cols // 2, 2, rows // cols * half, cols * here_k), BF16),
            pltpu.SemaphoreType.DMA((cols // 2,)),
        ],
        compiler_params=pltpu.CompilerParams(vmem_limit_bytes=VMEM_LIMIT),
        name="merge",
    )(left, own, other)


def gate_kernel(pair_ref, gain_ref, weight_ref, gate_ref):
    some, here_k, channels = pair_ref.shape
    rows = pair_ref[...].reshape(some * here_k, channels).astype(F32)
    normed = normalize(rows, gain_ref[...], 1)
    gate = sigmoid(jnp.dot(normed, weight_ref[...], preferred_element_type=F32))
    gate_ref[...] = gate.reshape(gate_ref.shape)


def gates(pair, gain, weight):
    here_i, here_k, channels = pair.shape
    some = here_i // 4
    block = pl.BlockSpec((some, here_k, channels), lambda i: (i, 0, 0))
    return pl.pallas_call(
        gate_kernel,
        grid=(4,),
        in_specs=[
            block,
            pl.BlockSpec(gain.shape, lambda i: (0, 0)),
            pl.BlockSpec(weight.shape, lambda i: (0, 0)),
        ],
        out_specs=block,
        out_shape=jax.ShapeDtypeStruct(pair.shape, F32),
        compiler_params=pltpu.CompilerParams(vmem_limit_bytes=VMEM_LIMIT),
        cost_estimate=pl.CostEstimate(
            flops=2 * pair.size * channels, bytes_accessed=6 * pair.size, transcendentals=pair.size
        ),
        name="gates",
    )(pair, gain, weight)


def update_kernel(
    odd_ref, back_ref, gain_ref, weight_ref, gate_ref, update_hbm, update_ref, left
):
    chips, cores, cols, half, here_k = back_ref.shape
    width, each = chips * cols, gate_ref.shape[1]
    channels = gate_ref.shape[4]
    odd = odd_ref[0]
    gain = jnp.broadcast_to(gain_ref[...], (here_k, width)).T.reshape(width, 1, here_k)
    outgoing = []
    for c in range(cores):
        product = back_ref[:, c].reshape(width, half, here_k).astype(F32)
        average = jnp.mean(product, axis=0, keepdims=True)
        centered = product - average
        spread = jnp.mean(centered * centered, axis=0, keepdims=True)
        normed = centered * lax.rsqrt(spread + 1e-05)
        normed = jnp.swapaxes((normed * gain).astype(BF16), 0, 1)
        first = (c + odd) % 2
        for i in range(half):
            row = c * half + i
            projected = lax.dot_general(
                normed[i], weight_ref[...], (((0,), (0,)), ((), ())), preferred_element_type=F32
            ).reshape(2, each, half, channels)
            update_ref[row, :, first] = (gate_ref[row, :, first] * projected[0]).astype(BF16)
            second = 1 - first
            update_ref[row, :, second] = (gate_ref[row, :, second] * projected[1]).astype(BF16)
            if (i + 1) % 4 == 0:
                span = pl.ds(row - 3, 4)
                copy = pltpu.make_async_copy(
                    update_ref.at[span], update_hbm.at[span], left.at[len(outgoing)]
                )
                copy.start()
                outgoing.append(copy)
    for copy in outgoing:
        copy.wait()


def updates(odd, back, gain, weight, gate):
    chips, _, cols, half, here_k = back.shape
    here_i, _, channels = gate.shape
    blocked = (here_i, here_k // (2 * half), 2, half, channels)
    vmem, hbm = pl.BlockSpec(memory_space=pltpu.VMEM), pl.BlockSpec(memory_space=pltpu.HBM)
    update = pl.pallas_call(
        update_kernel,
        in_specs=[pl.BlockSpec(memory_space=pltpu.SMEM), vmem, vmem, vmem, vmem],
        out_specs=hbm,
        out_shape=jax.ShapeDtypeStruct(blocked, BF16),
        scratch_shapes=[
            pltpu.VMEM(blocked, BF16),
            pltpu.SemaphoreType.DMA((here_i // 4,)),
        ],
        compiler_params=pltpu.CompilerParams(vmem_limit_bytes=VMEM_LIMIT),
        name="updates",
    )(odd, back, gain, weight, gate.reshape(blocked))
    return update.reshape(gate.shape)


def shards(rows, cols, pair, ln_in_gain, proj_left, proj_right, gate_weight, ln_out_gain, out_weight):
    width = out_weight.shape[0]
    here_i, here_k = pair.shape[0], pair.shape[1]
    half, chips = here_i // 2, rows // 2
    both = ("row", "col")
    exchange = functools.partial(
        lax.all_to_all, axis_name=both, split_axis=0, concat_axis=0, tiled=True
    )
    gain = ln_in_gain.reshape(1, -1)
    sent = operands(pair, gain, proj_left, proj_right, chips, cols)
    got = exchange(sent.reshape(rows * cols, 2, half, here_k))
    got = got.reshape(rows, cols, 2, half, here_k)
    other = lax.ppermute(split(got), "row", [(r, r ^ 1) for r in range(rows)])
    left, own = own_part(got)
    product = merge(left, own, other)
    product, late_pair = lax.optimization_barrier((product, pair))
    back = exchange(product.reshape(rows * cols, half, here_k))
    gate = gates(late_pair, gain, gate_weight)
    odd = lax.rem(lax.axis_index("col"), 2).reshape(1)
    return updates(
        odd, back.reshape(chips, 2, cols, half, here_k), ln_out_gain.reshape(1, width), out_weight, gate
    )


def solution(mesh):
    rows, cols = mesh.shape["row"], mesh.shape["col"]
    in_specs = (P("row", "col", None), P(), P(), P(), P(), P(), P())
    out_specs = P("row", "col", None)
    step = functools.partial(shards, rows, cols)
    return jax.shard_map(step, mesh=mesh, in_specs=in_specs, out_specs=out_specs, check_vma=False)
```

```python
import functools

import jax
import jax.numpy as jnp
from jax import lax
from jax.experimental import pallas as pl
from jax.experimental.pallas import tpu as pltpu
from jax.sharding import PartitionSpec as P

F32, BF16 = jnp.float32, jnp.bfloat16
VMEM_LIMIT = 40 * 1024 * 1024


def sigmoid(values):
    return 0.5 * jnp.tanh(0.5 * values) + 0.5


def normalize(values, gain, axis):
    average = jnp.mean(values, axis=axis, keepdims=True)
    centered = values - average
    spread = jnp.mean(centered * centered, axis=axis, keepdims=True)
    return (centered * lax.rsqrt(spread + 1e-05) * gain).astype(BF16)


PARTS = 2


def operands_kernel(
    pair_hbm, gain_hbm, left_hbm, right_hbm, sent_ref, pair_ref, gain_ref, weights, turned, sides, arrived
):
    here_i, here_k, channels = pair_ref.shape
    chips, cores, cols, _, half, _ = sent_ref.shape
    wide = left_hbm.shape[1]
    width, part = wide // 2, here_i // PARTS
    pieces = [
        pltpu.make_async_copy(
            pair_hbm.at[pl.ds(p * part, part)], pair_ref.at[pl.ds(p * part, part)], arrived.at[p]
        )
        for p in range(PARTS)
    ]
    small = [
        pltpu.make_async_copy(left_hbm, weights.at[0], arrived.at[PARTS]),
        pltpu.make_async_copy(right_hbm, weights.at[1], arrived.at[PARTS + 1]),
        pltpu.make_async_copy(gain_hbm, gain_ref, arrived.at[PARTS + 2]),
    ]
    for copy in pieces[:1] + small + pieces[1:]:
        copy.start()
    for copy in small + pieces[:1]:
        copy.wait()
    for side in range(2):
        turned[side * wide : (side + 1) * wide] = (0.5 * weights[side].astype(F32)).T.astype(BF16)
    gain = jnp.broadcast_to(gain_ref[...], (2 * here_k, channels)).T
    for core in range(cores):
        for i in range(0, half, 2):
            row = core * half + i
            if row % part == 0 and row > 0:
                pieces[row // part].wait()
            turned_rows = pair_ref[row : row + 2].reshape(2 * here_k, channels).T.astype(F32)
            normed = normalize(turned_rows, gain, 0)
            both = lax.dot_general(
                turned[...], normed, (((1,), (0,)), ((), ())), preferred_element_type=F32
            )
            for side in range(2):
                one = both[side * wide : (side + 1) * wide]
                gated = (jnp.tanh(one[:width]) + 1.0) * one[width:]
                sides[core, side, i] = gated[:, :here_k]
                sides[core, side, i + 1] = gated[:, here_k:]
        for side in range(2):
            by_channel = jnp.swapaxes(sides[core, side], 0, 1).astype(BF16)
            sent_ref[:, core, :, side] = by_channel.reshape(chips, cols, half, here_k)


def operands(pair, gain, proj_left, proj_right, chips, cols):
    here_i, here_k, channels = pair.shape
    half, wide = here_i // 2, proj_left.shape[1]
    hbm = pl.BlockSpec(memory_space=pltpu.HBM)
    arrays = [
        pltpu.with_memory_space_constraint(array, pltpu.HBM)
        for array in (pair, gain, proj_left, proj_right)
    ]
    return pl.pallas_call(
        operands_kernel,
        in_specs=[hbm] * 4,
        out_specs=pl.BlockSpec(memory_space=pltpu.VMEM),
        out_shape=jax.ShapeDtypeStruct((chips, 2, cols, 2, half, here_k), BF16),
        scratch_shapes=[
            pltpu.VMEM(pair.shape, BF16),
            pltpu.VMEM(gain.shape, F32),
            pltpu.VMEM((2, channels, wide), BF16),
            pltpu.VMEM((2 * wide, channels), BF16),
            pltpu.VMEM((2, 2, half, wide // 2, here_k), F32),
            pltpu.SemaphoreType.DMA((PARTS + 3,)),
        ],
        compiler_params=pltpu.CompilerParams(vmem_limit_bytes=VMEM_LIMIT),
        name="operands",
    )(*arrays)


def split_kernel(got_ref, right_ref):
    rows, cols, _, half, here_k = got_ref.shape
    for s in range(cols):
        right_ref[:, s * here_k : (s + 1) * here_k] = got_ref[:, s, 1].reshape(rows * half, here_k)


def split(got):
    rows, cols, _, half, here_k = got.shape
    vmem = pl.BlockSpec(memory_space=pltpu.VMEM)
    return pl.pallas_call(
        split_kernel,
        in_specs=[vmem],
        out_specs=vmem,
        out_shape=jax.ShapeDtypeStruct((rows * half, cols * here_k), BF16),
        compiler_params=pltpu.CompilerParams(vmem_limit_bytes=VMEM_LIMIT),
        name="split",
    )(got)


def own_kernel(got_ref, right_ref, left_ref, own_ref):
    rows, cols, _, half, here_k = got_ref.shape
    for s in range(cols):
        span = pl.ds(s * here_k, here_k)
        left_ref[:, span] = got_ref[:, s, 0].reshape(rows * half, here_k)
    step = 2 * here_k
    for j in range(0, rows * half, step):
        own_ref[:, j : j + step] = lax.dot_general(
            left_ref[...], right_ref[j : j + step], (((1,), (1,)), ((), ())), preferred_element_type=F32
        ).astype(BF16)


def own_part(got, right):
    rows, cols, _, half, here_k = got.shape
    tall, deep = rows * half, cols * here_k
    vmem = pl.BlockSpec(memory_space=pltpu.VMEM)
    return pl.pallas_call(
        own_kernel,
        in_specs=[vmem, vmem],
        out_specs=[vmem, vmem],
        out_shape=[
            jax.ShapeDtypeStruct((tall, deep), BF16),
            jax.ShapeDtypeStruct((tall, tall), BF16),
        ],
        compiler_params=pltpu.CompilerParams(vmem_limit_bytes=VMEM_LIMIT),
        cost_estimate=pl.CostEstimate(
            flops=2 * tall * tall * deep, bytes_accessed=8 * tall * deep, transcendentals=0
        ),
        name="own_part",
    )(got, right)


def merge_kernel(left_ref, own_ref, other_ref, product_hbm, product_ref, left):
    rows, cols, half, here_k = product_ref.shape
    each = rows // cols * half
    outgoing = []
    first = lax.broadcasted_iota(jnp.int32, (1, here_k), 1) < each
    for pair in range(0, cols // 2, 2):
        part = jnp.concatenate(
            [
                other_ref[s * each : (s + 1) * each]
                for s in (2 * pair + 1, 2 * pair, 2 * pair + 3, 2 * pair + 2)
            ]
        )
        total = lax.dot_general(
            left_ref[...], part, (((1,), (1,)), ((), ())), preferred_element_type=F32
        )
        for p in range(2):
            span = pl.ds((pair + p) * here_k, here_k)
            own = own_ref[:, span].astype(F32)
            other = total[:, p * here_k : (p + 1) * here_k]
            even = jnp.where(first, own, other).astype(BF16)
            odd = jnp.where(first, other, own).astype(BF16)
            product_ref[:, 2 * (pair + p)] = even.reshape(rows, half, here_k)
            product_ref[:, 2 * (pair + p) + 1] = odd.reshape(rows, half, here_k)
            span = pl.ds(2 * (pair + p), 2)
            copy = pltpu.make_async_copy(
                product_ref.at[:, span], product_hbm.at[:, span], left.at[pair + p]
            )
            copy.start()
            outgoing.append(copy)
    for copy in outgoing:
        copy.wait()


def merge(left, own, other, shape):
    cols = shape[1]
    vmem = pl.BlockSpec(memory_space=pltpu.VMEM)
    return pl.pallas_call(
        merge_kernel,
        in_specs=[vmem, vmem, vmem],
        out_specs=pl.BlockSpec(memory_space=pltpu.HBM),
        out_shape=jax.ShapeDtypeStruct(shape, BF16),
        scratch_shapes=[
            pltpu.VMEM(shape, BF16),
            pltpu.SemaphoreType.DMA((cols // 2,)),
        ],
        compiler_params=pltpu.CompilerParams(vmem_limit_bytes=VMEM_LIMIT),
        name="merge",
    )(left, own, other)


def gate_kernel(pair_ref, gain_ref, weight_ref, gate_ref):
    some, here_k, channels = pair_ref.shape
    rows = pair_ref[...].reshape(some * here_k, channels).astype(F32)
    normed = normalize(rows, gain_ref[...], 1)
    gate = sigmoid(jnp.dot(normed, weight_ref[...], preferred_element_type=F32))
    gate_ref[...] = gate.reshape(gate_ref.shape)


def gates(pair, gain, weight):
    here_i, here_k, channels = pair.shape
    some = here_i // 4
    block = pl.BlockSpec((some, here_k, channels), lambda i: (i, 0, 0))
    return pl.pallas_call(
        gate_kernel,
        grid=(4,),
        in_specs=[
            block,
            pl.BlockSpec(gain.shape, lambda i: (0, 0)),
            pl.BlockSpec(weight.shape, lambda i: (0, 0)),
        ],
        out_specs=block,
        out_shape=jax.ShapeDtypeStruct(pair.shape, F32),
        compiler_params=pltpu.CompilerParams(vmem_limit_bytes=VMEM_LIMIT),
        cost_estimate=pl.CostEstimate(
            flops=2 * pair.size * channels, bytes_accessed=6 * pair.size, transcendentals=pair.size
        ),
        name="gates",
    )(pair, gain, weight)


def update_kernel(
    odd_ref, back_ref, gain_ref, weight_ref, gate_ref, update_hbm, update_ref, left
):
    chips, cores, cols, half, here_k = back_ref.shape
    width, each = chips * cols, gate_ref.shape[1]
    channels = gate_ref.shape[4]
    odd = odd_ref[0]
    gain = jnp.broadcast_to(gain_ref[...], (here_k, width)).T.reshape(width, 1, here_k)
    outgoing = []
    for c in range(cores):
        product = back_ref[:, c].reshape(width, half, here_k).astype(F32)
        average = jnp.mean(product, axis=0, keepdims=True)
        centered = product - average
        spread = jnp.mean(centered * centered, axis=0, keepdims=True)
        normed = centered * lax.rsqrt(spread + 1e-05)
        normed = jnp.swapaxes((normed * gain).astype(BF16), 0, 1)
        first = (c + odd) % 2
        for i in range(half):
            row = c * half + i
            projected = lax.dot_general(
                normed[i], weight_ref[...], (((0,), (0,)), ((), ())), preferred_element_type=F32
            ).reshape(2, each, half, channels)
            update_ref[row, :, first] = (gate_ref[row, :, first] * projected[0]).astype(BF16)
            second = 1 - first
            update_ref[row, :, second] = (gate_ref[row, :, second] * projected[1]).astype(BF16)
            if (i + 1) % 4 == 0:
                span = pl.ds(row - 3, 4)
                copy = pltpu.make_async_copy(
                    update_ref.at[span], update_hbm.at[span], left.at[len(outgoing)]
                )
                copy.start()
                outgoing.append(copy)
    for copy in outgoing:
        copy.wait()


def updates(odd, back, gain, weight, gate):
    chips, _, cols, half, here_k = back.shape
    here_i, _, channels = gate.shape
    blocked = (here_i, here_k // (2 * half), 2, half, channels)
    vmem, hbm = pl.BlockSpec(memory_space=pltpu.VMEM), pl.BlockSpec(memory_space=pltpu.HBM)
    update = pl.pallas_call(
        update_kernel,
        in_specs=[pl.BlockSpec(memory_space=pltpu.SMEM), vmem, vmem, vmem, vmem],
        out_specs=hbm,
        out_shape=jax.ShapeDtypeStruct(blocked, BF16),
        scratch_shapes=[
            pltpu.VMEM(blocked, BF16),
            pltpu.SemaphoreType.DMA((here_i // 4,)),
        ],
        compiler_params=pltpu.CompilerParams(vmem_limit_bytes=VMEM_LIMIT),
        name="updates",
    )(odd, back, gain, weight, gate.reshape(blocked))
    return update.reshape(gate.shape)


def shards(rows, cols, pair, ln_in_gain, proj_left, proj_right, gate_weight, ln_out_gain, out_weight):
    width = out_weight.shape[0]
    here_i, here_k = pair.shape[0], pair.shape[1]
    half, chips = here_i // 2, rows // 2
    both = ("row", "col")
    exchange = functools.partial(
        lax.all_to_all, axis_name=both, split_axis=0, concat_axis=0, tiled=True
    )
    gain = ln_in_gain.reshape(1, -1)
    sent = operands(pair, gain, proj_left, proj_right, chips, cols)
    got = exchange(sent.reshape(rows * cols, 2, half, here_k))
    got = got.reshape(rows, cols, 2, half, here_k)
    right = split(got)
    other = lax.ppermute(right, "row", [(r, r ^ 1) for r in range(rows)])
    left, own = own_part(got, right)
    product = merge(left, own, other, (rows, cols, half, here_k))
    product, late_pair = lax.optimization_barrier((product, pair))
    back = exchange(product.reshape(rows * cols, half, here_k))
    gate = gates(late_pair, gain, gate_weight)
    odd = lax.rem(lax.axis_index("col"), 2).reshape(1)
    return updates(
        odd, back.reshape(chips, 2, cols, half, here_k), ln_out_gain.reshape(1, width), out_weight, gate
    )


def solution(mesh):
    rows, cols = mesh.shape["row"], mesh.shape["col"]
    in_specs = (P("row", "col", None), P(), P(), P(), P(), P(), P())
    out_specs = P("row", "col", None)
    step = functools.partial(shards, rows, cols)
    return jax.shard_map(step, mesh=mesh, in_specs=in_specs, out_specs=out_specs, check_vma=False)
```

```python
import functools

import jax
import jax.numpy as jnp
from jax import lax
from jax.experimental import pallas as pl
from jax.experimental.pallas import tpu as pltpu
from jax.sharding import PartitionSpec as P

F32, BF16 = jnp.float32, jnp.bfloat16
VMEM_LIMIT = 40 * 1024 * 1024


def normalize(values, gain, axis):
    average = jnp.mean(values, axis=axis, keepdims=True)
    centered = values - average
    spread = jnp.mean(centered * centered, axis=axis, keepdims=True)
    return (centered * lax.rsqrt(spread + 1e-05) * gain).astype(BF16)


PARTS = 2


def operands_kernel(
    pair_hbm, gain_hbm, left_hbm, right_hbm, sent_ref, pair_ref, gain_ref, weights, turned, sides, arrived
):
    here_i, here_k, channels = pair_ref.shape
    chips, cores, cols, _, half, _ = sent_ref.shape
    wide = left_hbm.shape[1]
    width, part = wide // 2, here_i // PARTS
    pieces = [
        pltpu.make_async_copy(
            pair_hbm.at[pl.ds(p * part, part)], pair_ref.at[pl.ds(p * part, part)], arrived.at[p]
        )
        for p in range(PARTS)
    ]
    small = [
        pltpu.make_async_copy(left_hbm, weights.at[0], arrived.at[PARTS]),
        pltpu.make_async_copy(right_hbm, weights.at[1], arrived.at[PARTS + 1]),
        pltpu.make_async_copy(gain_hbm, gain_ref, arrived.at[PARTS + 2]),
    ]
    for copy in pieces[:1] + small + pieces[1:]:
        copy.start()
    for copy in small + pieces[:1]:
        copy.wait()
    for side in range(2):
        turned[side * wide : (side + 1) * wide] = (0.5 * weights[side].astype(F32)).T.astype(BF16)
    gain = jnp.broadcast_to(gain_ref[...], (2 * here_k, channels)).T
    for core in range(cores):
        for i in range(0, half, 2):
            row = core * half + i
            if row % part == 0 and row > 0:
                pieces[row // part].wait()
            turned_rows = pair_ref[row : row + 2].reshape(2 * here_k, channels).T.astype(F32)
            normed = normalize(turned_rows, gain, 0)
            both = lax.dot_general(
                turned[...], normed, (((1,), (0,)), ((), ())), preferred_element_type=F32
            )
            for side in range(2):
                one = both[side * wide : (side + 1) * wide]
                gated = (jnp.tanh(one[:width]) + 1.0) * one[width:]
                sides[core, side, i] = gated[:, :here_k]
                sides[core, side, i + 1] = gated[:, here_k:]
        for side in range(2):
            by_channel = jnp.swapaxes(sides[core, side], 0, 1).astype(BF16)
            sent_ref[:, core, :, side] = by_channel.reshape(chips, cols, half, here_k)


def operands(pair, gain, proj_left, proj_right, chips, cols):
    here_i, here_k, channels = pair.shape
    half, wide = here_i // 2, proj_left.shape[1]
    hbm = pl.BlockSpec(memory_space=pltpu.HBM)
    arrays = [
        pltpu.with_memory_space_constraint(array, pltpu.HBM)
        for array in (pair, gain, proj_left, proj_right)
    ]
    return pl.pallas_call(
        operands_kernel,
        in_specs=[hbm] * 4,
        out_specs=pl.BlockSpec(memory_space=pltpu.VMEM),
        out_shape=jax.ShapeDtypeStruct((chips, 2, cols, 2, half, here_k), BF16),
        scratch_shapes=[
            pltpu.VMEM(pair.shape, BF16),
            pltpu.VMEM(gain.shape, F32),
            pltpu.VMEM((2, channels, wide), BF16),
            pltpu.VMEM((2 * wide, channels), BF16),
            pltpu.VMEM((2, 2, half, wide // 2, here_k), F32),
            pltpu.SemaphoreType.DMA((PARTS + 3,)),
        ],
        compiler_params=pltpu.CompilerParams(vmem_limit_bytes=VMEM_LIMIT),
        name="operands",
    )(*arrays)


def split_kernel(got_ref, right_ref):
    rows, cols, _, half, here_k = got_ref.shape
    for s in range(cols):
        right_ref[:, s * here_k : (s + 1) * here_k] = got_ref[:, s, 1].reshape(rows * half, here_k)


def split(got):
    rows, cols, _, half, here_k = got.shape
    vmem = pl.BlockSpec(memory_space=pltpu.VMEM)
    return pl.pallas_call(
        split_kernel,
        in_specs=[vmem],
        out_specs=vmem,
        out_shape=jax.ShapeDtypeStruct((rows * half, cols * here_k), BF16),
        compiler_params=pltpu.CompilerParams(vmem_limit_bytes=VMEM_LIMIT),
        name="split",
    )(got)


def own_kernel(
    got_ref, right_ref, pair_hbm, gain_hbm, weight_hbm, last_gain_hbm, last_weight_hbm,
    left_ref, own_ref, gate_ref, columns_ref, halved_ref,
    pair_ref, gain_ref, weight_ref, last_gain_ref, last_weight_ref, arrived,
):
    incoming = [
        pltpu.make_async_copy(source, target, arrived.at[n])
        for n, (source, target) in enumerate(
            (
                (weight_hbm, weight_ref),
                (gain_hbm, gain_ref),
                (pair_hbm, pair_ref),
                (last_gain_hbm, last_gain_ref),
                (last_weight_hbm, last_weight_ref),
            )
        )
    ]
    for copy in incoming:
        copy.start()
    rows, cols, _, half, here_k = got_ref.shape
    for s in range(cols):
        span = pl.ds(s * here_k, here_k)
        left_ref[:, span] = got_ref[:, s, 0].reshape(rows * half, here_k)
    step = 2 * here_k
    for j in range(0, rows * half, step):
        own_ref[:, j : j + step] = lax.dot_general(
            left_ref[...], right_ref[j : j + step], (((1,), (1,)), ((), ())), preferred_element_type=F32
        ).astype(BF16)
    for copy in incoming:
        copy.wait()
    weight = (0.5 * weight_ref[...].astype(F32)).astype(BF16)
    halved_ref[...] = (0.5 * last_weight_ref[...].astype(F32)).astype(BF16)
    columns_ref[...] = jnp.broadcast_to(last_gain_ref[...], columns_ref.shape[::-1]).T
    here_i, _, channels = pair_ref.shape
    for i in range(0, here_i, 4):
        some = pair_ref[i : i + 4].reshape(4 * here_k, channels).astype(F32)
        gate = jnp.dot(normalize(some, gain_ref[...], 1), weight, preferred_element_type=F32)
        gate_ref[i : i + 4] = (jnp.tanh(gate) + 1.0).reshape(4, here_k, channels)


def own_part(got, right, pair, gain, gate_weight, last_gain, last_weight):
    rows, cols, _, half, here_k = got.shape
    tall, deep = rows * half, cols * here_k
    vmem, hbm = pl.BlockSpec(memory_space=pltpu.VMEM), pl.BlockSpec(memory_space=pltpu.HBM)
    arrays = [
        pltpu.with_memory_space_constraint(array, pltpu.HBM)
        for array in (pair, gain, gate_weight, last_gain, last_weight)
    ]
    return pl.pallas_call(
        own_kernel,
        in_specs=[vmem] * 2 + [hbm] * 5,
        out_specs=[vmem] * 5,
        out_shape=[
            jax.ShapeDtypeStruct((tall, deep), BF16),
            jax.ShapeDtypeStruct((tall, tall), BF16),
            jax.ShapeDtypeStruct(pair.shape, F32),
            jax.ShapeDtypeStruct((last_gain.shape[1], here_k), F32),
            jax.ShapeDtypeStruct(last_weight.shape, BF16),
        ],
        scratch_shapes=[
            pltpu.VMEM(pair.shape, BF16),
            pltpu.VMEM(gain.shape, F32),
            pltpu.VMEM(gate_weight.shape, BF16),
            pltpu.VMEM(last_gain.shape, F32),
            pltpu.VMEM(last_weight.shape, BF16),
            pltpu.SemaphoreType.DMA((5,)),
        ],
        compiler_params=pltpu.CompilerParams(vmem_limit_bytes=VMEM_LIMIT),
        cost_estimate=pl.CostEstimate(
            flops=2 * tall * tall * deep, bytes_accessed=8 * tall * deep, transcendentals=0
        ),
        name="own_part",
    )(got, right, *arrays)


def merge_kernel(left_ref, own_ref, other_ref, product_ref):
    rows, cols, half, here_k = product_ref.shape
    each = rows // cols * half
    first = lax.broadcasted_iota(jnp.int32, (1, here_k), 1) < each
    for pair in range(0, cols // 2, 2):
        part = jnp.concatenate(
            [
                other_ref[s * each : (s + 1) * each]
                for s in (2 * pair + 1, 2 * pair, 2 * pair + 3, 2 * pair + 2)
            ]
        )
        total = lax.dot_general(
            left_ref[...], part, (((1,), (1,)), ((), ())), preferred_element_type=F32
        )
        for p in range(2):
            span = pl.ds((pair + p) * here_k, here_k)
            own = own_ref[:, span].astype(F32)
            other = total[:, p * here_k : (p + 1) * here_k]
            even = jnp.where(first, own, other).astype(BF16)
            odd = jnp.where(first, other, own).astype(BF16)
            product_ref[:, 2 * (pair + p)] = even.reshape(rows, half, here_k)
            product_ref[:, 2 * (pair + p) + 1] = odd.reshape(rows, half, here_k)


def merge(left, own, other, shape):
    vmem = pl.BlockSpec(memory_space=pltpu.VMEM)
    return pl.pallas_call(
        merge_kernel,
        in_specs=[vmem, vmem, vmem],
        out_specs=vmem,
        out_shape=jax.ShapeDtypeStruct(shape, BF16),
        compiler_params=pltpu.CompilerParams(vmem_limit_bytes=VMEM_LIMIT),
        name="merge",
    )(left, own, other)


def update_kernel(
    odd_ref, back_ref, gain_ref, weight_ref, gate_ref, update_hbm, update_ref, left
):
    chips, cores, cols, half, here_k = back_ref.shape
    width, each = chips * cols, gate_ref.shape[1]
    channels = gate_ref.shape[4]
    odd = odd_ref[0]
    gain = gain_ref[...].reshape(width, 1, here_k)
    outgoing = []
    for c in range(cores):
        product = back_ref[:, c].reshape(width, half, here_k).astype(F32)
        average = jnp.mean(product, axis=0, keepdims=True)
        centered = product - average
        spread = jnp.mean(centered * centered, axis=0, keepdims=True)
        normed = centered * lax.rsqrt(spread + 1e-05)
        normed = jnp.swapaxes((normed * gain).astype(BF16), 0, 1)
        first = (c + odd) % 2
        for i in range(half):
            row = c * half + i
            projected = lax.dot_general(
                normed[i], weight_ref[...], (((0,), (0,)), ((), ())), preferred_element_type=F32
            ).reshape(2, each, half, channels)
            update_ref[row, :, first] = (gate_ref[row, :, first] * projected[0]).astype(BF16)
            second = 1 - first
            update_ref[row, :, second] = (gate_ref[row, :, second] * projected[1]).astype(BF16)
            if (i + 1) % 4 == 0:
                span = pl.ds(row - 3, 4)
                copy = pltpu.make_async_copy(
                    update_ref.at[span], update_hbm.at[span], left.at[len(outgoing)]
                )
                copy.start()
                outgoing.append(copy)
    for copy in outgoing:
        copy.wait()


def updates(odd, back, gain, weight, gate):
    chips, _, cols, half, here_k = back.shape
    here_i, _, channels = gate.shape
    blocked = (here_i, here_k // (2 * half), 2, half, channels)
    vmem, hbm = pl.BlockSpec(memory_space=pltpu.VMEM), pl.BlockSpec(memory_space=pltpu.HBM)
    update = pl.pallas_call(
        update_kernel,
        in_specs=[pl.BlockSpec(memory_space=pltpu.SMEM), vmem, vmem, vmem, vmem],
        out_specs=hbm,
        out_shape=jax.ShapeDtypeStruct(blocked, BF16),
        scratch_shapes=[
            pltpu.VMEM(blocked, BF16),
            pltpu.SemaphoreType.DMA((here_i // 4,)),
        ],
        compiler_params=pltpu.CompilerParams(vmem_limit_bytes=VMEM_LIMIT),
        name="updates",
    )(odd, back, gain, weight, gate.reshape(blocked))
    return update.reshape(gate.shape)


def shards(rows, cols, pair, ln_in_gain, proj_left, proj_right, gate_weight, ln_out_gain, out_weight):
    width = out_weight.shape[0]
    here_i, here_k = pair.shape[0], pair.shape[1]
    half, chips = here_i // 2, rows // 2
    both = ("row", "col")
    exchange = functools.partial(
        lax.all_to_all, axis_name=both, split_axis=0, concat_axis=0, tiled=True
    )
    gain = ln_in_gain.reshape(1, -1)
    sent = operands(pair, gain, proj_left, proj_right, chips, cols)
    got = exchange(sent.reshape(rows * cols, 2, half, here_k))
    got = got.reshape(rows, cols, 2, half, here_k)
    right = split(got)
    other = lax.ppermute(right, "row", [(r, r ^ 1) for r in range(rows)])
    left, own, gate, columns, halved = own_part(
        got, right, pair, gain, gate_weight, ln_out_gain.reshape(1, width), out_weight
    )
    product = merge(left, own, other, (rows, cols, half, here_k))
    odd = lax.rem(lax.axis_index("col"), 2).reshape(1)
    product, odd = lax.optimization_barrier((product, odd))
    back = exchange(product.reshape(rows * cols, half, here_k))
    return updates(odd, back.reshape(chips, 2, cols, half, here_k), columns, halved, gate)


def solution(mesh):
    rows, cols = mesh.shape["row"], mesh.shape["col"]
    in_specs = (P("row", "col", None), P(), P(), P(), P(), P(), P())
    out_specs = P("row", "col", None)
    step = functools.partial(shards, rows, cols)
    return jax.shard_map(step, mesh=mesh, in_specs=in_specs, out_specs=out_specs, check_vma=False)
```
